32 devices in a mesh: dp: 2 (over core), seq: 16 (over z, y, x).
Axes of the slice: x: 2, y: 2, z: 4, core: 2. Of those that a mesh axis runs over, the one named last changes fastest.
Arguments:
- self_query: bfloat16 [2, 2048, 4096], P('dp', 'seq'), may hold values from -120 to 120
- self_key: bfloat16 [2, 2048, 4096], P('dp', 'seq'), may hold values from -6 to 6
- self_value: bfloat16 [2, 2048, 4096], P('dp', 'seq'), may hold values from -6 to 6
- cross_query: bfloat16 [2, 2048, 4096], P('dp', 'seq'), may hold values from -250 to 250
- text_embed: bfloat16 [2, 16, 512, 4096], P('dp', 'seq'), may hold values from -6 to 6
- cross_key_weight: bfloat16 [4096, 4096], P('dp', 'seq'), may hold values from -0.09375 to 0.09375
- cross_value_weight: bfloat16 [4096, 4096], P('dp', 'seq'), may hold values from -0.09375 to 0.09375
- text_lengths: int32 [2], P('dp'), may hold values from 64 to 512, as said below
- encoder_index: int32 [2], P('dp'), may hold values from 0 to 15
Outputs:
- attended: bfloat16 [2, 2048, 4096], P('dp', 'seq')
The draws below stay inside these ranges and needn't reach their ends.
Inputs may be any that keep to these rules, and one draw needn't show every extreme that they name: `text_lengths`: one clip's prompt fills all 512 positions and another clip's holds 64.
All inputs are finite; a program needn't handle non-finite values.
Results may differ from the reference program's by a relative error of at most 0.011.
Values may be sent and summed in bfloat16 or wider, within the bound.
No kernel may reach another device: no remote copies, remote signals or barrier semaphores. Data moves between devices by JAX's collectives and lax.ppermute only.
A program may use at most 128 MiB of HBM per device.

```python
import jax
import jax.numpy as jnp
from jax import lax

HEADS = 32
HEAD = 128
TEXT = 512
EMB = 4096
SEQ = 2048
CLIPS = 2
N_SEQ = 16


def shared_keys(key):
    base = jax.random.normal(jax.random.fold_in(key, 97), (CLIPS, SEQ, HEADS * HEAD), jnp.float32)
    return jnp.clip(base, -6.0, 6.0)


def draw_self_key(key, part):
    key = jax.random.fold_in(key, 1)
    base = shared_keys(key_base(key))
    return base.astype(jnp.bfloat16)


def key_base(key):
    return jax.random.fold_in(key, 0)


def draw_self_query(key, part):
    key = jax.random.fold_in(key, 2)
    fresh = jnp.clip(jax.random.normal(key, (CLIPS, SEQ, HEADS * HEAD), jnp.float32), -6.0, 6.0)
    return fresh.astype(jnp.bfloat16)


def draw_cross_query(key, part):
    key = jax.random.fold_in(key, 3)
    fresh = jnp.clip(jax.random.normal(key, (CLIPS, SEQ, HEADS * HEAD), jnp.float32), -6.0, 6.0)
    return fresh.astype(jnp.bfloat16)


def draw_text_lengths(key, part):
    key = jax.random.fold_in(key, 5)
    first, second = jax.random.split(key)
    lengths = jax.random.randint(first, (CLIPS,), TEXT // 8, TEXT + 1, dtype=jnp.int32)
    pick = jax.random.randint(second, (), 0, CLIPS, dtype=jnp.int32)
    slots = jnp.arange(CLIPS, dtype=jnp.int32)
    lengths = jnp.where(slots == pick, jnp.int32(TEXT), lengths)
    lengths = jnp.where(slots == (pick + 1) % CLIPS, jnp.int32(TEXT // 8), lengths)
    return lengths.astype(jnp.int32)


def level_of(rng, shape, cuts, smallest, top_value):
    factor_of, own = 1.0, jax.random.fold_in(rng, 6)
    for position, blocks in cuts:
        steps = jnp.exp(jax.random.uniform(jax.random.fold_in(own, position), (blocks,), jnp.float32, smallest / len(cuts), top_value / len(cuts)))
        factor_of = factor_of * jnp.repeat(steps, shape[position] // blocks).reshape([-1 if axis == position else 1 for axis in range(len(shape))])
    return factor_of


def normal_values(rng, dims, scale, most, shards=(), kind=jnp.bfloat16):
    loudness = level_of(rng, dims, shards, -0.22, 0.18) if shards else 1.0
    drawn = jax.random.normal(rng, dims, jnp.float32) * scale * loudness
    return jnp.minimum(jnp.maximum(drawn, -most), most).astype(kind)


def setup_inputs(seed: int = 0) -> dict:
    arg_keys = jax.random.split(jax.random.key(seed), 10)
    return {
        "self_query": draw_self_query(jax.random.fold_in(arg_keys[9], 71), 0),
        "self_key": draw_self_key(jax.random.fold_in(arg_keys[9], 71), 0),
        "self_value": normal_values(arg_keys[2], (CLIPS, SEQ, HEADS * HEAD), 1.0, 6.0, ((0, 2), (1, 16))),
        "cross_query": draw_cross_query(jax.random.fold_in(arg_keys[9], 71), 0),
        "text_embed": normal_values(arg_keys[4], (CLIPS, N_SEQ, TEXT, EMB), 1.0, 6.0, ((0, 2), (1, 16))),
        "cross_key_weight": normal_values(arg_keys[5], (EMB, HEADS * HEAD), EMB ** -0.5, 0.09375, ((0, 2), (1, 16))),
        "cross_value_weight": normal_values(arg_keys[6], (EMB, HEADS * HEAD), EMB ** -0.5, 0.09375, ((0, 2), (1, 16))),
        "text_lengths": draw_text_lengths(jax.random.fold_in(arg_keys[9], 71), 0),
        "encoder_index": jax.random.randint(arg_keys[8], (CLIPS,), 0, N_SEQ).astype(jnp.int32),
    }


def attend_all(queries, keys, values, bias):
    rows = queries.shape[0]
    block = min(512, rows)
    scale = 1.0 / (queries.shape[2] ** 0.5)

    def one_block(query_rows):
        scores = jnp.einsum("qhe,khe->hqk", query_rows, keys, preferred_element_type=jnp.float32) * scale + bias
        top = jnp.max(scores, axis=2, keepdims=True)
        probs = jnp.exp(scores - top)
        total = jnp.sum(probs, axis=2, keepdims=True)
        weights = (probs / total).astype(jnp.bfloat16)
        return jnp.einsum("hqk,khe->qhe", weights, values, preferred_element_type=jnp.float32)

    blocks = queries.reshape(rows // block, block, queries.shape[1], queries.shape[2])
    outputs = lax.map(one_block, blocks)
    return outputs.reshape(rows, queries.shape[1], queries.shape[2]).astype(jnp.bfloat16)


def reference(self_query, self_key, self_value, cross_query, text_embed, cross_key_weight, cross_value_weight, text_lengths, encoder_index):
    def one_clip(items):
        query, key_rows, value_rows, cross_rows, slots, length, owner = items
        prompt = lax.dynamic_index_in_dim(slots, owner, 0, keepdims=False)
        cross_key = jnp.dot(prompt, cross_key_weight, preferred_element_type=jnp.float32).astype(jnp.bfloat16)
        cross_value = jnp.dot(prompt, cross_value_weight, preferred_element_type=jnp.float32).astype(jnp.bfloat16)
        shape = (SEQ, HEADS, HEAD)
        self_out = attend_all(query.reshape(shape), key_rows.reshape(shape), value_rows.reshape(shape), jnp.float32(0.0))
        valid = jnp.arange(TEXT, dtype=jnp.int32) < length
        bias = jnp.where(valid, jnp.float32(0.0), jnp.float32(-1e30))[None, None, :]
        text_shape = (TEXT, HEADS, HEAD)
        cross_out = attend_all(cross_rows.reshape(shape), cross_key.reshape(text_shape), cross_value.reshape(text_shape), bias)
        both = self_out.astype(jnp.float32) + cross_out.astype(jnp.float32)
        return both.astype(jnp.bfloat16).reshape(SEQ, HEADS * HEAD)

    return lax.map(one_clip, (self_query, self_key, self_value, cross_query, text_embed, text_lengths, encoder_index))
```

```python
import functools
import math

import jax
import jax.numpy as jnp
from jax import lax
from jax.experimental import pallas as pl
from jax.experimental.pallas import tpu as pltpu
from jax.sharding import PartitionSpec as P

HEAD = 128
VMEM_BYTES = 48 * 1024 * 1024
LOG2E = math.log2(math.e)


def params():
    return pltpu.CompilerParams(vmem_limit_bytes=VMEM_BYTES)


def pack(arrays, n):
    rows, columns = arrays[0].shape
    width = columns // n
    per = max(1, n // 4)
    count = len(arrays)

    def body(*refs):
        out_ref = refs[-1]
        for a in range(count):
            for j in range(per):
                out_ref[j, a] = refs[a][:, j * width : (j + 1) * width]

    return pl.pallas_call(
        body,
        grid=(n // per,),
        in_specs=[pl.BlockSpec((rows, per * width), lambda i: (0, i))] * count,
        out_specs=pl.BlockSpec((per, count, rows, width), lambda i: (i, 0, 0, 0)),
        out_shape=jax.ShapeDtypeStruct((n, count, rows, width), arrays[0].dtype),
        compiler_params=params(),
        name="pack",
    )(*arrays)


def unpack(blocks):
    n, rows, width = blocks.shape
    per = max(1, n // 4)

    def body(in_ref, out_ref):
        for j in range(per):
            out_ref[:, j * width : (j + 1) * width] = in_ref[j]

    return pl.pallas_call(
        body,
        grid=(n // per,),
        in_specs=[pl.BlockSpec((per, rows, width), lambda i: (i, 0, 0))],
        out_specs=pl.BlockSpec((rows, per * width), lambda i: (0, i)),
        out_shape=jax.ShapeDtypeStruct((rows, n * width), blocks.dtype),
        compiler_params=params(),
        name="unpack",
    )(blocks)


def self_attention(blocks):
    n, _, rows, width = blocks.shape
    heads = width // HEAD
    tokens = n * rows
    per = max(1, min(n, 256 // rows))
    step = 2 * per if n % (2 * per) == 0 else per
    factor = LOG2E / HEAD**0.5

    def body(q_ref, k_ref, v_ref, out_ref, values):
        @pl.when(pl.program_id(1) == 0)
        def _():
            values[:, :HEAD] = v_ref[:, 0].reshape(tokens, HEAD)
            values[:, HEAD:] = jnp.ones((tokens, HEAD), jnp.bfloat16)

        keys = k_ref[:, 0].reshape(tokens, HEAD)
        for part in range(step // per):
            q = q_ref[part * per : (part + 1) * per, 0].reshape(per * rows, HEAD)
            scores = lax.dot_general(
                q, keys, (((1,), (1,)), ((), ())), preferred_element_type=jnp.float32
            )
            top = jnp.max(scores, axis=1, keepdims=True)
            probs = jnp.exp2((scores - top) * factor).astype(jnp.bfloat16)
            total = jnp.dot(probs, values[...], preferred_element_type=jnp.float32)
            out = (total[:, :HEAD] / total[:, HEAD:]).astype(jnp.bfloat16)
            out_ref[part * per : (part + 1) * per] = out.reshape(per, rows, HEAD)

    return pl.pallas_call(
        body,
        grid=(heads, n // step),
        in_specs=[
            pl.BlockSpec((step, 1, rows, HEAD), lambda h, i: (i, 0, 0, h)),
            pl.BlockSpec((n, 1, rows, HEAD), lambda h, i: (0, 1, 0, h)),
            pl.BlockSpec((n, 1, rows, HEAD), lambda h, i: (0, 2, 0, h)),
        ],
        out_specs=pl.BlockSpec((step, rows, HEAD), lambda h, i: (i, 0, h)),
        out_shape=jax.ShapeDtypeStruct((n, rows, width), jnp.bfloat16),
        scratch_shapes=[pltpu.VMEM((tokens, 2 * HEAD), jnp.bfloat16)],
        compiler_params=params(),
        cost_estimate=pl.CostEstimate(
            flops=4 * heads * tokens * tokens * HEAD,
            bytes_accessed=2 * 4 * tokens * width,
            transcendentals=heads * tokens * tokens,
        ),
        name="self_attention",
    )(blocks, blocks, blocks)


def cross_attention(queries, text, length, self_out):
    n, rows, width = queries.shape
    heads = width // HEAD
    positions = text.shape[0]
    step = max(1, min(n, 512 // rows))
    factor = LOG2E / HEAD**0.5

    def body(length_ref, q_ref, k_ref, v_ref, self_ref, out_ref, values):
        @pl.when(pl.program_id(1) == 0)
        def _():
            values[:, :HEAD] = v_ref[...]
            values[:, HEAD:] = jnp.ones((positions, HEAD), jnp.bfloat16)

        q = q_ref[...].reshape(step * rows, HEAD)
        scores = lax.dot_general(
            q, k_ref[...], (((1,), (1,)), ((), ())), preferred_element_type=jnp.float32
        )
        place = lax.broadcasted_iota(jnp.int32, (1, positions), 1)
        scores = jnp.where(place < length_ref[0], scores, -1e30)
        top = jnp.max(scores, axis=1, keepdims=True)
        probs = jnp.exp2((scores - top) * factor).astype(jnp.bfloat16)
        total = jnp.dot(probs, values[...], preferred_element_type=jnp.float32)
        out = (total[:, :HEAD] / total[:, HEAD:]).astype(jnp.bfloat16).astype(jnp.float32)
        out = out.reshape(step, rows, HEAD) + self_ref[...].astype(jnp.float32)
        out_ref[...] = out.astype(jnp.bfloat16)

    return pl.pallas_call(
        body,
        grid_spec=pltpu.PrefetchScalarGridSpec(
            num_scalar_prefetch=1,
            grid=(heads, n // step),
            in_specs=[
                pl.BlockSpec((step, rows, HEAD), lambda h, i, _: (i, 0, h)),
                pl.BlockSpec((positions, HEAD), lambda h, i, _: (0, h)),
                pl.BlockSpec((positions, HEAD), lambda h, i, _: (0, heads + h)),
                pl.BlockSpec((step, rows, HEAD), lambda h, i, _: (i, 0, h)),
            ],
            out_specs=pl.BlockSpec((step, rows, HEAD), lambda h, i, _: (i, 0, h)),
            scratch_shapes=[pltpu.VMEM((positions, 2 * HEAD), jnp.bfloat16)],
        ),
        out_shape=jax.ShapeDtypeStruct((n, rows, width), jnp.bfloat16),
        compiler_params=params(),
        cost_estimate=pl.CostEstimate(
            flops=4 * heads * n * rows * positions * HEAD,
            bytes_accessed=2 * 3 * n * rows * width,
            transcendentals=heads * n * rows * positions,
        ),
        name="cross_attention",
    )(length, queries, text, text, self_out)


def exchange(value, bit, n):
    return lax.ppermute(value, "seq", [(i, i ^ (1 << bit)) for i in range(n)])


def swap(value):
    return lax.ppermute(value, "dp", [(0, 1), (1, 0)])


def bit_of(index, bit):
    return (index >> bit) & 1


def pick(value, index):
    return lax.dynamic_index_in_dim(value, index, 0, keepdims=False)


def in_order(mine, other, position):
    first = jnp.where(position == 0, mine, other)
    second = jnp.where(position == 0, other, mine)
    return jnp.stack([first, second])


def text_of_pair(embed, key_weight, value_weight, length, encoder, n):
    positions, columns = embed.shape
    few = positions // 8
    core = lax.axis_index("dp")
    me = lax.axis_index("seq")
    half = columns // 2
    facts = jnp.stack([length, encoder])
    other_facts = swap(facts)
    own_half = lax.dynamic_slice_in_dim(embed, core * half, half, 1)
    sent_half = lax.dynamic_slice_in_dim(embed, (1 - core) * half, half, 1)
    other_half = swap(sent_half)
    mine_long = length > other_facts[0]
    encoder_long = jnp.where(mine_long, encoder, other_facts[1])
    encoder_short = jnp.where(mine_long, other_facts[1], encoder)
    long = jnp.where(mine_long, own_half, other_half)
    short = jnp.where(mine_long, other_half[:few], own_half[:few])
    rows_long, rows_short = positions // 4, few // 4
    rows = rows_long + rows_short
    packed = jnp.concatenate(
        [long.reshape(4, rows_long, half), short.reshape(4, rows_short, half)], axis=1
    ).reshape(2, 2, rows, half)

    def choose(own, got, bit):
        keep_long = bit_of(encoder_long, bit) == bit_of(me, bit)
        keep_short = bit_of(encoder_short, bit) == bit_of(me, bit)
        place = lax.broadcasted_iota(jnp.int32, (rows, 1), 0)
        keep = jnp.where(place < rows_long, keep_long, keep_short)
        return jnp.where(keep, own, got)

    x, y = bit_of(me, 0), bit_of(me, 1)
    part_a, part_b = packed[..., : half // 2], packed[..., half // 2 :]
    part_a, part_b = part_a.transpose(1, 0, 2, 3), part_b
    got_a = exchange(pick(part_a, 1 - x), 0, n)
    got_b = exchange(pick(part_b, 1 - y), 1, n)
    part_a = choose(pick(part_a, x), got_a, 0)
    part_b = choose(pick(part_b, y), got_b, 1)
    got_a = exchange(pick(part_a, 1 - y), 1, n)
    got_b = exchange(pick(part_b, 1 - x), 0, n)
    piece = jnp.concatenate(
        [choose(pick(part_a, y), got_a, 1), choose(pick(part_b, x), got_b, 0)], axis=1
    )
    bits = n.bit_length() - 1
    last = bits - 1
    for bit in range(2, last):
        piece = choose(piece, exchange(piece, bit, n), bit)
    near = bit_of(me, 2)
    halves = jnp.stack([piece[:, : half // 2], piece[:, half // 2 :]])
    own = pick(halves, near)
    own = choose(own, exchange(own, last, n), last)
    got = exchange(own, 2, n)
    part_a, part_b = jnp.where(near == 0, own, got), jnp.where(near == 0, got, own)
    two_a = in_order(part_a, exchange(part_a, 1, n), y)
    two_b = in_order(part_b, exchange(part_b, 0, n), x)
    four_a = in_order(two_a, exchange(two_a, 0, n), x).transpose(1, 0, 2, 3)
    four_b = in_order(two_b, exchange(two_b, 1, n), y)
    weight = jnp.concatenate([key_weight, value_weight], axis=1)
    width = weight.shape[1]
    sums = jnp.dot(
        four_a.reshape(4 * rows, half // 2), weight[: half // 2], preferred_element_type=jnp.float32
    ) + jnp.dot(
        four_b.reshape(4 * rows, half // 2), weight[half // 2 :], preferred_element_type=jnp.float32
    )
    sums = sums.reshape(4, rows, width)
    sums_long = sums[:, :rows_long].reshape(positions, width)
    sums_short = jnp.pad(sums[:, rows_long:].reshape(few, width), ((0, positions - few), (0, 0)))
    mine = jnp.where(mine_long, sums_long, sums_short)
    sent = jnp.where(mine_long, sums_short, sums_long)
    return (mine + swap(sent)).astype(jnp.bfloat16)


def text_of_clip(embed, key_weight, value_weight, encoder):
    kept = jnp.where(lax.axis_index("seq") == encoder, embed, 0).astype(embed.dtype)
    prompt = lax.psum(kept, "seq")
    weight = lax.all_gather(
        jnp.concatenate([key_weight, value_weight], axis=1), "dp", axis=0, tiled=True
    )
    return jnp.dot(prompt, weight, preferred_element_type=jnp.float32).astype(jnp.bfloat16)


def shards(
    n_dp,
    n,
    self_query,
    self_key,
    self_value,
    cross_query,
    text_embed,
    cross_key_weight,
    cross_value_weight,
    text_lengths,
    encoder_index,
):
    packed = pack([self_query[0], self_key[0], self_value[0]], n)
    count, rows, width = packed.shape[1:]
    packed_cross = pack([cross_query[0]], n).reshape(n, rows, width)
    blocks = lax.all_to_all(
        packed.reshape(n, count * rows, width), "seq", split_axis=0, concat_axis=0, tiled=True
    ).reshape(packed.shape)
    packed_cross, blocks = lax.optimization_barrier((packed_cross, blocks))
    cross = lax.all_to_all(packed_cross, "seq", split_axis=0, concat_axis=0, tiled=True)
    if n_dp == 2 and n >= 16 and n & (n - 1) == 0:
        text = text_of_pair(
            text_embed[0, 0],
            cross_key_weight,
            cross_value_weight,
            text_lengths[0],
            encoder_index[0],
            n,
        )
    else:
        text = text_of_clip(
            text_embed[0, 0], cross_key_weight, cross_value_weight, encoder_index[0]
        )
    self_out = self_attention(blocks)
    out = cross_attention(cross, text, text_lengths, self_out)
    tokens = lax.all_to_all(out, "seq", split_axis=0, concat_axis=0, tiled=True)
    return unpack(tokens)[None]


def solution(mesh):
    placed = (
        P("dp", "seq", None),
        P("dp", "seq", None),
        P("dp", "seq", None),
        P("dp", "seq", None),
        P("dp", "seq", None, None),
        P("dp", "seq"),
        P("dp", "seq"),
        P("dp"),
        P("dp"),
    )
    return jax.shard_map(
        functools.partial(shards, mesh.shape["dp"], mesh.shape["seq"]),
        mesh=mesh,
        in_specs=placed,
        out_specs=P("dp", "seq", None),
        check_vma=False,
    )
```

```python
import functools
import math

import jax
import jax.numpy as jnp
from jax import lax
from jax.experimental import pallas as pl
from jax.experimental.pallas import tpu as pltpu
from jax.sharding import PartitionSpec as P

HEAD = 128
VMEM_BYTES = 48 * 1024 * 1024
LOG2E = math.log2(math.e)


def params():
    return pltpu.CompilerParams(vmem_limit_bytes=VMEM_BYTES)


def pack(arrays, n, groups):
    rows, columns = arrays[0].shape
    width = columns // n
    part = width // groups
    per = max(1, n // 4)
    count = len(arrays)

    def body(*refs):
        for g in range(groups):
            for a in range(count):
                for j in range(per):
                    start = j * width + g * part
                    refs[count + g][j, a] = refs[a][:, start : start + part]

    return pl.pallas_call(
        body,
        grid=(n // per,),
        in_specs=[pl.BlockSpec((rows, per * width), lambda i: (0, i))] * count,
        out_specs=[pl.BlockSpec((per, count, rows, part), lambda i: (i, 0, 0, 0))] * groups,
        out_shape=[jax.ShapeDtypeStruct((n, count, rows, part), arrays[0].dtype)] * groups,
        compiler_params=params(),
        name="pack",
    )(*arrays)


def unpack(parts):
    groups = len(parts)
    n, rows, part = parts[0].shape
    width = part * groups
    per = max(1, n // 4)

    def body(*refs):
        for g in range(groups):
            for j in range(per):
                start = j * width + g * part
                refs[groups][:, start : start + part] = refs[g][j]

    return pl.pallas_call(
        body,
        grid=(n // per,),
        in_specs=[pl.BlockSpec((per, rows, part), lambda i: (i, 0, 0))] * groups,
        out_specs=pl.BlockSpec((rows, per * width), lambda i: (0, i)),
        out_shape=jax.ShapeDtypeStruct((rows, n * width), parts[0].dtype),
        compiler_params=params(),
        name="unpack",
    )(*parts)


def self_attention(blocks):
    n, _, rows, width = blocks.shape
    heads = width // HEAD
    tokens = n * rows
    per = max(1, min(n, 256 // rows))
    step = 2 * per if n % (2 * per) == 0 else per
    factor = LOG2E / HEAD**0.5

    def body(q_ref, k_ref, v_ref, out_ref, values):
        @pl.when(pl.program_id(1) == 0)
        def _():
            values[:, :HEAD] = v_ref[:, 0].reshape(tokens, HEAD)
            values[:, HEAD:] = jnp.ones((tokens, HEAD), jnp.bfloat16)

        keys = k_ref[:, 0].reshape(tokens, HEAD)
        for part in range(step // per):
            q = q_ref[part * per : (part + 1) * per, 0].reshape(per * rows, HEAD)
            scores = lax.dot_general(
                q, keys, (((1,), (1,)), ((), ())), preferred_element_type=jnp.float32
            )
            top = jnp.max(scores, axis=1, keepdims=True)
            probs = jnp.exp2((scores - top) * factor).astype(jnp.bfloat16)
            total = jnp.dot(probs, values[...], preferred_element_type=jnp.float32)
            out = (total[:, :HEAD] / total[:, HEAD:]).astype(jnp.bfloat16)
            out_ref[part * per : (part + 1) * per] = out.reshape(per, rows, HEAD)

    return pl.pallas_call(
        body,
        grid=(heads, n // step),
        in_specs=[
            pl.BlockSpec((step, 1, rows, HEAD), lambda h, i: (i, 0, 0, h)),
            pl.BlockSpec((n, 1, rows, HEAD), lambda h, i: (0, 1, 0, h)),
            pl.BlockSpec((n, 1, rows, HEAD), lambda h, i: (0, 2, 0, h)),
        ],
        out_specs=pl.BlockSpec((step, rows, HEAD), lambda h, i: (i, 0, h)),
        out_shape=jax.ShapeDtypeStruct((n, rows, width), jnp.bfloat16),
        scratch_shapes=[pltpu.VMEM((tokens, 2 * HEAD), jnp.bfloat16)],
        compiler_params=params(),
        cost_estimate=pl.CostEstimate(
            flops=4 * heads * tokens * tokens * HEAD,
            bytes_accessed=2 * 4 * tokens * width,
            transcendentals=heads * tokens * tokens,
        ),
        name="self_attention",
    )(blocks, blocks, blocks)


def cross_attention(blocks, text, length, self_out, first):
    n, _, rows, width = blocks.shape
    heads = width // HEAD
    positions = text.shape[0]
    values_at = text.shape[1] // HEAD // 2 + first
    step = max(1, min(n, 512 // rows))
    factor = LOG2E / HEAD**0.5

    def body(length_ref, q_ref, k_ref, v_ref, self_ref, out_ref, values):
        @pl.when(pl.program_id(1) == 0)
        def _():
            values[:, :HEAD] = v_ref[...]
            values[:, HEAD:] = jnp.ones((positions, HEAD), jnp.bfloat16)

        q = q_ref[:, 0].reshape(step * rows, HEAD)
        scores = lax.dot_general(
            q, k_ref[...], (((1,), (1,)), ((), ())), preferred_element_type=jnp.float32
        )
        place = lax.broadcasted_iota(jnp.int32, (1, positions), 1)
        scores = jnp.where(place < length_ref[0], scores, -1e30)
        top = jnp.max(scores, axis=1, keepdims=True)
        probs = jnp.exp2((scores - top) * factor).astype(jnp.bfloat16)
        total = jnp.dot(probs, values[...], preferred_element_type=jnp.float32)
        out = (total[:, :HEAD] / total[:, HEAD:]).astype(jnp.bfloat16).astype(jnp.float32)
        out = out.reshape(step, rows, HEAD) + self_ref[...].astype(jnp.float32)
        out_ref[...] = out.astype(jnp.bfloat16)

    return pl.pallas_call(
        body,
        grid_spec=pltpu.PrefetchScalarGridSpec(
            num_scalar_prefetch=1,
            grid=(heads, n // step),
            in_specs=[
                pl.BlockSpec((step, 1, rows, HEAD), lambda h, i, _: (i, 3, 0, h)),
                pl.BlockSpec((positions, HEAD), lambda h, i, _: (0, first + h)),
                pl.BlockSpec((positions, HEAD), lambda h, i, _: (0, values_at + h)),
                pl.BlockSpec((step, rows, HEAD), lambda h, i, _: (i, 0, h)),
            ],
            out_specs=pl.BlockSpec((step, rows, HEAD), lambda h, i, _: (i, 0, h)),
            scratch_shapes=[pltpu.VMEM((positions, 2 * HEAD), jnp.bfloat16)],
        ),
        out_shape=jax.ShapeDtypeStruct((n, rows, width), jnp.bfloat16),
        compiler_params=params(),
        cost_estimate=pl.CostEstimate(
            flops=4 * heads * n * rows * positions * HEAD,
            bytes_accessed=2 * 3 * n * rows * width,
            transcendentals=heads * n * rows * positions,
        ),
        name="cross_attention",
    )(length, blocks, text, text, self_out)


def spread(blocks):
    flat = blocks.reshape(blocks.shape[0], -1, blocks.shape[-1])
    return lax.all_to_all(flat, "seq", split_axis=0, concat_axis=0, tiled=True).reshape(blocks.shape)


def exchange(value, bit, n):
    return lax.ppermute(value, "seq", [(i, i ^ (1 << bit)) for i in range(n)])


def swap(value):
    return lax.ppermute(value, "dp", [(0, 1), (1, 0)])


def bit_of(index, bit):
    return (index >> bit) & 1


def pick(value, index):
    return lax.dynamic_index_in_dim(value, index, 0, keepdims=False)


def in_order(mine, other, position):
    first = jnp.where(position == 0, mine, other)
    second = jnp.where(position == 0, other, mine)
    return jnp.stack([first, second])


def text_of_pair(embed, key_weight, value_weight, length, encoder, n, before, between):
    positions, columns = embed.shape
    few = positions // 8
    core = lax.axis_index("dp")
    me = lax.axis_index("seq")
    half = columns // 2
    facts = jnp.stack([length, encoder])
    other_facts = swap(facts)
    own_half = lax.dynamic_slice_in_dim(embed, core * half, half, 1)
    sent_half = lax.dynamic_slice_in_dim(embed, (1 - core) * half, half, 1)
    other_half = swap(sent_half)
    mine_long = length > other_facts[0]
    encoder_long = jnp.where(mine_long, encoder, other_facts[1])
    encoder_short = jnp.where(mine_long, other_facts[1], encoder)
    long = jnp.where(mine_long, own_half, other_half)
    short = jnp.where(mine_long, other_half[:few], own_half[:few])
    rows_long, rows_short = positions // 4, few // 4
    rows = rows_long + rows_short
    packed = jnp.concatenate(
        [long.reshape(4, rows_long, half), short.reshape(4, rows_short, half)], axis=1
    ).reshape(2, 2, rows, half)

    def choose(own, got, bit):
        keep_long = bit_of(encoder_long, bit) == bit_of(me, bit)
        keep_short = bit_of(encoder_short, bit) == bit_of(me, bit)
        place = lax.broadcasted_iota(jnp.int32, (rows, 1), 0)
        keep = jnp.where(place < rows_long, keep_long, keep_short)
        return jnp.where(keep, own, got)

    x, y = bit_of(me, 0), bit_of(me, 1)
    part_a, part_b = packed[..., : half // 2], packed[..., half // 2 :]
    part_a, part_b = part_a.transpose(1, 0, 2, 3), part_b
    got_a = exchange(pick(part_a, 1 - x), 0, n)
    got_b = exchange(pick(part_b, 1 - y), 1, n)
    part_a = choose(pick(part_a, x), got_a, 0)
    part_b = choose(pick(part_b, y), got_b, 1)
    got_a = exchange(pick(part_a, 1 - y), 1, n)
    got_b = exchange(pick(part_b, 1 - x), 0, n)
    piece = jnp.concatenate(
        [choose(pick(part_a, y), got_a, 1), choose(pick(part_b, x), got_b, 0)], axis=1
    )
    piece = before(piece)
    bits = n.bit_length() - 1
    last = bits - 1
    for bit in range(2, last):
        piece = choose(piece, exchange(piece, bit, n), bit)
    near = bit_of(me, 2)
    halves = jnp.stack([piece[:, : half // 2], piece[:, half // 2 :]])
    own = pick(halves, near)
    own = choose(own, exchange(own, last, n), last)
    got = exchange(own, 2, n)
    part_a, part_b = jnp.where(near == 0, own, got), jnp.where(near == 0, got, own)
    part_a, part_b = between((part_a, part_b))
    two_a = in_order(part_a, exchange(part_a, 1, n), y)
    two_b = in_order(part_b, exchange(part_b, 0, n), x)
    four_a = in_order(two_a, exchange(two_a, 0, n), x).transpose(1, 0, 2, 3)
    four_b = in_order(two_b, exchange(two_b, 1, n), y)
    weight = jnp.concatenate([key_weight, value_weight], axis=1)
    width = weight.shape[1]
    sums = jnp.dot(
        four_a.reshape(4 * rows, half // 2), weight[: half // 2], preferred_element_type=jnp.float32
    ) + jnp.dot(
        four_b.reshape(4 * rows, half // 2), weight[half // 2 :], preferred_element_type=jnp.float32
    )
    sums = sums.reshape(4, rows, width)
    sums_long = sums[:, :rows_long].reshape(positions, width)
    sums_short = jnp.pad(sums[:, rows_long:].reshape(few, width), ((0, positions - few), (0, 0)))
    mine = jnp.where(mine_long, sums_long, sums_short)
    sent = jnp.where(mine_long, sums_short, sums_long)
    return (mine + swap(sent)).astype(jnp.bfloat16)


def text_of_clip(embed, key_weight, value_weight, encoder):
    kept = jnp.where(lax.axis_index("seq") == encoder, embed, 0).astype(embed.dtype)
    prompt = lax.psum(kept, "seq")
    weight = lax.all_gather(
        jnp.concatenate([key_weight, value_weight], axis=1), "dp", axis=0, tiled=True
    )
    return jnp.dot(prompt, weight, preferred_element_type=jnp.float32).astype(jnp.bfloat16)


def shards(
    n_dp,
    n,
    self_query,
    self_key,
    self_value,
    cross_query,
    text_embed,
    cross_key_weight,
    cross_value_weight,
    text_lengths,
    encoder_index,
):
    width = cross_key_weight.shape[1]
    groups = 2 if width // HEAD % 2 == 0 else 1
    packed = pack([self_query[0], self_key[0], self_value[0], cross_query[0]], n, groups)
    blocks = [spread(packed[0])]
    self_out = []
    pair = n_dp == 2 and n >= 16 and n & (n - 1) == 0

    def before(piece):
        blocks[0], piece = lax.optimization_barrier((blocks[0], piece))
        self_out.append(self_attention(blocks[0]))
        return piece

    def between(parts):
        if groups > 1:
            parts, later, self_out[0] = lax.optimization_barrier((parts, packed[1], self_out[0]))
            blocks.append(spread(later))
        return parts

    if pair:
        text = text_of_pair(
            text_embed[0, 0],
            cross_key_weight,
            cross_value_weight,
            text_lengths[0],
            encoder_index[0],
            n,
            before,
            between,
        )
    else:
        before(text_lengths)
        between(text_lengths)
        text = text_of_clip(
            text_embed[0, 0], cross_key_weight, cross_value_weight, encoder_index[0]
        )
    tokens = []
    for g in range(groups):
        if g > 0:
            blocks[g], out = lax.optimization_barrier((blocks[g], out))
            self_out.append(self_attention(blocks[g]))
            tokens.append(spread(out))
        first = g * (width // HEAD // groups)
        out = cross_attention(blocks[g], text, text_lengths, self_out[g], first)
    tokens.append(spread(out))
    return unpack(tokens)[None]


def solution(mesh):
    placed = (
        P("dp", "seq", None),
        P("dp", "seq", None),
        P("dp", "seq", None),
        P("dp", "seq", None),
        P("dp", "seq", None, None),
        P("dp", "seq"),
        P("dp", "seq"),
        P("dp"),
        P("dp"),
    )
    return jax.shard_map(
        functools.partial(shards, mesh.shape["dp"], mesh.shape["seq"]),
        mesh=mesh,
        in_specs=placed,
        out_specs=P("dp", "seq", None),
        check_vma=False,
    )
```

```python
import functools
import math

import jax
import jax.numpy as jnp
from jax import lax
from jax.experimental import pallas as pl
from jax.experimental.pallas import tpu as pltpu
from jax.sharding import PartitionSpec as P

HEAD = 128
QUAD = 4
LOG2E = math.log2(math.e)


def params(mebibytes=48):
    return pltpu.CompilerParams(vmem_limit_bytes=mebibytes * 1024 * 1024)


def pack(arrays, n, items, part):
    rows, columns = arrays[0].shape
    width = columns // n
    per = max(1, n // 4)
    used = sorted({a for a, _ in items})

    def body(*refs):
        for i, (a, g) in enumerate(items):
            for j in range(per):
                start = j * width + g * part
                refs[-1][j, i] = refs[used.index(a)][:, start : start + part]

    return pl.pallas_call(
        body,
        grid=(n // per,),
        in_specs=[pl.BlockSpec((rows, per * width), lambda i: (0, i))] * len(used),
        out_specs=pl.BlockSpec((per, len(items), rows, part), lambda i: (i, 0, 0, 0)),
        out_shape=jax.ShapeDtypeStruct((n, len(items), rows, part), arrays[0].dtype),
        compiler_params=params(60),
        name="pack",
    )(*[arrays[a] for a in used])


def unpack(parts):
    groups = len(parts)
    n, rows, part = parts[0].shape
    width = part * groups
    per = max(1, n // 4)

    def body(*refs):
        for g in range(groups):
            for j in range(per):
                start = j * width + g * part
                refs[groups][:, start : start + part] = refs[g][j]

    return pl.pallas_call(
        body,
        grid=(n // per,),
        in_specs=[pl.BlockSpec((per, rows, part), lambda i: (i, 0, 0))] * groups,
        out_specs=pl.BlockSpec((rows, per * width), lambda i: (0, i)),
        out_shape=jax.ShapeDtypeStruct((rows, n * width), parts[0].dtype),
        compiler_params=params(),
        name="unpack",
    )(*parts)


def result_blocks(n, step, rows, turned):
    if turned:
        lines = n // QUAD
        return (lines, QUAD, rows), pl.BlockSpec(
            (lines, 1, rows, HEAD), lambda h, i, *_: (0, i, 0, h)
        )
    return (n // step, step, rows), pl.BlockSpec(
        (1, step, rows, HEAD), lambda h, i, *_: (i, 0, 0, h)
    )


def self_attention(blocks, first, turned):
    n, _, rows, width = blocks.shape
    heads = width // HEAD
    tokens = n * rows
    per = max(1, min(n, 256 // rows))
    step = n // QUAD if turned else 2 * per
    factor = LOG2E / HEAD**0.5
    shape, out_block = result_blocks(n, step, rows, turned)

    def body(q_ref, k_ref, v_ref, out_ref, values):
        @pl.when(pl.program_id(1) == 0)
        def _():
            values[:, :HEAD] = v_ref[:, 0].reshape(tokens, HEAD)
            values[:, HEAD:] = jnp.ones((tokens, HEAD), jnp.bfloat16)

        keys = k_ref[:, 0].reshape(tokens, HEAD)
        outs = []
        for part in range(step // per):
            q = q_ref[part * per : (part + 1) * per, 0].reshape(per * rows, HEAD)
            scores = lax.dot_general(
                q, keys, (((1,), (1,)), ((), ())), preferred_element_type=jnp.float32
            )
            top = jnp.max(scores, axis=1, keepdims=True)
            probs = jnp.exp2((scores - top) * factor).astype(jnp.bfloat16)
            total = jnp.dot(probs, values[...], preferred_element_type=jnp.float32)
            outs.append((total[:, :HEAD] / total[:, HEAD:]).astype(jnp.bfloat16))
        out_ref[...] = jnp.concatenate(outs).reshape(out_ref.shape)

    return pl.pallas_call(
        body,
        grid=(heads, n // step),
        in_specs=[
            pl.BlockSpec((step, 1, rows, HEAD), lambda h, i: (i, first, 0, h)),
            pl.BlockSpec((n, 1, rows, HEAD), lambda h, i: (0, first + 1, 0, h)),
            pl.BlockSpec((n, 1, rows, HEAD), lambda h, i: (0, first + 2, 0, h)),
        ],
        out_specs=out_block,
        out_shape=jax.ShapeDtypeStruct((*shape, width), jnp.bfloat16),
        scratch_shapes=[pltpu.VMEM((tokens, 2 * HEAD), jnp.bfloat16)],
        compiler_params=params(),
        cost_estimate=pl.CostEstimate(
            flops=16 * heads * tokens * tokens * HEAD,
            bytes_accessed=2 * 4 * tokens * width,
            transcendentals=heads * tokens * tokens,
        ),
        name="self_attention",
    )(blocks, blocks, blocks).reshape(n, rows, width)


def cross_attention(blocks, item, text, head, length, self_out):
    n, _, rows, width = blocks.shape
    heads = width // HEAD
    positions = text.shape[0]
    values_at = text.shape[1] // HEAD // 2 + head
    step = max(1, min(n, 512 // rows))
    factor = LOG2E / HEAD**0.5
    self_block = pl.BlockSpec((step, rows, HEAD), lambda h, i, _: (i, 0, h))

    def body(length_ref, q_ref, k_ref, v_ref, self_ref, out_ref, values):
        @pl.when(pl.program_id(1) == 0)
        def _():
            values[:, :HEAD] = v_ref[...]
            values[:, HEAD:] = jnp.ones((positions, HEAD), jnp.bfloat16)

        q = q_ref[:, 0].reshape(step * rows, HEAD)
        scores = lax.dot_general(
            q, k_ref[...], (((1,), (1,)), ((), ())), preferred_element_type=jnp.float32
        )
        place = lax.broadcasted_iota(jnp.int32, (1, positions), 1)
        scores = jnp.where(place < length_ref[0], scores, -1e30)
        top = jnp.max(scores, axis=1, keepdims=True)
        probs = jnp.exp2((scores - top) * factor).astype(jnp.bfloat16)
        total = jnp.dot(probs, values[...], preferred_element_type=jnp.float32)
        out = (total[:, :HEAD] / total[:, HEAD:]).astype(jnp.bfloat16).astype(jnp.float32)
        out = out.reshape(self_ref.shape) + self_ref[...].astype(jnp.float32)
        out_ref[...] = out.astype(jnp.bfloat16)

    return pl.pallas_call(
        body,
        grid_spec=pltpu.PrefetchScalarGridSpec(
            num_scalar_prefetch=1,
            grid=(heads, n // step),
            in_specs=[
                pl.BlockSpec((step, 1, rows, HEAD), lambda h, i, _: (i, item, 0, h)),
                pl.BlockSpec((positions, HEAD), lambda h, i, _: (0, head + h)),
                pl.BlockSpec((positions, HEAD), lambda h, i, _: (0, values_at + h)),
                self_block,
            ],
            out_specs=self_block,
            scratch_shapes=[pltpu.VMEM((positions, 2 * HEAD), jnp.bfloat16)],
        ),
        out_shape=jax.ShapeDtypeStruct((n, rows, width), jnp.bfloat16),
        compiler_params=params(),
        cost_estimate=pl.CostEstimate(
            flops=32 * heads * n * rows * positions * HEAD,
            bytes_accessed=2 * 3 * n * rows * width,
            transcendentals=heads * n * rows * positions,
        ),
        name="cross_attention",
    )(length, blocks, text, text, self_out)


def spread(blocks, groups=None):
    flat = blocks.reshape(blocks.shape[0], -1, blocks.shape[-1])
    return lax.all_to_all(
        flat, "seq", split_axis=0, concat_axis=0, tiled=True, axis_index_groups=groups
    ).reshape(blocks.shape)


def spread_lines(blocks):
    n = blocks.shape[0]
    return spread(blocks, [[q + QUAD * z for z in range(n // QUAD)] for q in range(QUAD)])


def spread_planes(blocks):
    n = blocks.shape[0]
    shape = blocks.shape[1:]
    turned = blocks.reshape(n // QUAD, QUAD, *shape).swapaxes(0, 1).reshape(n, *shape)
    return spread(turned, [[QUAD * z + q for q in range(QUAD)] for z in range(n // QUAD)])


def exchange(value, apart, n):
    return lax.ppermute(value, "seq", [(i, i ^ apart) for i in range(n)])


def pick(value, index):
    return lax.dynamic_index_in_dim(value, index, 0, keepdims=False)


def swap(value):
    return lax.ppermute(value, "dp", [(0, 1), (1, 0)])


def quarters(embed, other, where):
    positions, columns = embed.shape
    rows_long, rows_short = positions // 4, positions // 32
    rows = rows_long + rows_short
    half, part = columns // 2, columns // 4

    def body(where_ref, own_ref, other_ref, send_a, keep_a, send_b, keep_b):
        x, y = where_ref[2] & 1, where_ref[2] >> 1

        def fill(long_ref, short_ref):
            for i in range(2):
                for ref, place, first in (
                    (send_a, 2 * i + 1 - x, 0),
                    (keep_a, 2 * i + x, 0),
                    (send_b, 2 * (1 - y) + i, part),
                    (keep_b, 2 * y + i, part),
                ):
                    across = slice(first, first + part)
                    at_long = pl.ds(pl.multiple_of(place * rows_long, rows_long), rows_long)
                    at_short = pl.ds(pl.multiple_of(place * rows_short, rows_short), rows_short)
                    ref[i, :rows_long] = long_ref[at_long, across]
                    ref[i, rows_long:] = short_ref[at_short, across]

        @pl.when(where_ref[1] == 1)
        def _():
            fill(own_ref, other_ref)

        @pl.when(where_ref[1] == 0)
        def _():
            fill(other_ref, own_ref)

    return pl.pallas_call(
        body,
        grid_spec=pltpu.PrefetchScalarGridSpec(
            num_scalar_prefetch=1,
            grid=(1,),
            in_specs=[pl.BlockSpec((positions, half), lambda i, w: (0, w[0]))] * 2,
            out_specs=[pl.BlockSpec((2, rows, part), lambda i, w: (0, 0, 0))] * 4,
        ),
        out_shape=[jax.ShapeDtypeStruct((2, rows, part), embed.dtype)] * 4,
        compiler_params=params(),
        name="quarters",
    )(where, embed, other)


def project(pieces, key_weight, value_weight, where, positions):
    rows, columns = pieces[0].shape
    width = key_weight.shape[1]
    half = columns // 2
    rows_long, rows_short = positions // 4, positions // 32

    def body(where_ref, *refs):
        piece_refs, (key_ref, value_ref, mine_ref, sent_ref) = refs[:5], refs[5:]
        halves = [(ref[:, :half], ref[:, half:]) for ref in piece_refs[:3]]
        halves.append((piece_refs[3][...], piece_refs[4][...]))

        def fill(long_ref, short_ref):
            short_ref[4 * rows_short :] = jnp.zeros(
                (positions - 4 * rows_short, 2 * width), jnp.float32
            )
            near = where_ref[2]
            first = pl.ds(pl.multiple_of(near * half, half), half)
            second = pl.ds(pl.multiple_of((1 - near) * half, half), half)
            for i, (left, right) in enumerate(halves):
                place = where_ref[0] ^ i
                at_long = pl.ds(pl.multiple_of(place * rows_long, rows_long), rows_long)
                at_short = pl.ds(pl.multiple_of(place * rows_short, rows_short), rows_short)
                for j, ref in enumerate((key_ref, value_ref)):
                    sums = jnp.dot(left, ref[first], preferred_element_type=jnp.float32)
                    sums += jnp.dot(right, ref[second], preferred_element_type=jnp.float32)
                    across = slice(j * width, (j + 1) * width)
                    long_ref[at_long, across] = sums[:rows_long]
                    short_ref[at_short, across] = sums[rows_long:]

        @pl.when(where_ref[1] == 1)
        def _():
            fill(mine_ref, sent_ref)

        @pl.when(where_ref[1] == 0)
        def _():
            fill(sent_ref, mine_ref)

    def whole(*shape):
        return pl.BlockSpec(shape, lambda i, w: (0, 0))

    return pl.pallas_call(
        body,
        grid_spec=pltpu.PrefetchScalarGridSpec(
            num_scalar_prefetch=1,
            grid=(1,),
            in_specs=[whole(rows, columns)] * 3
            + [whole(rows, half)] * 2
            + [whole(columns, width)] * 2,
            out_specs=[whole(positions, 2 * width)] * 2,
        ),
        out_shape=[jax.ShapeDtypeStruct((positions, 2 * width), jnp.float32)] * 2,
        compiler_params=params(),
        name="project",
    )(where, *pieces, key_weight, value_weight)


def text_of_pair(embed, key_weight, value_weight, length, encoder, n, before, between, after):
    positions, columns = embed.shape
    core = lax.axis_index("dp")
    me = lax.axis_index("seq")
    half = columns // 2
    other = swap(embed)
    other_facts = swap(jnp.stack([length, encoder]))
    mine_long = length > other_facts[0]
    encoder_long = jnp.where(mine_long, encoder, other_facts[1])
    encoder_short = jnp.where(mine_long, other_facts[1], encoder)
    rows_long, rows_short = positions // 4, positions // 32
    rows = rows_long + rows_short
    place = me & 3
    is_long = mine_long.astype(jnp.int32)
    send_a, part_a, send_b, part_b = quarters(embed, other, jnp.stack([core, is_long, place]))
    on_row = lax.broadcasted_iota(jnp.int32, (rows, 1), 0)
    apart = jnp.where(on_row < rows_long, encoder_long, encoder_short) ^ me
    x, y = me & 1, (me >> 1) & 1

    def choose(own, got, bit):
        return jnp.where((apart >> bit) & 1 == 0, own, got)

    part_a = choose(part_a, exchange(send_a, 1, n), 0)
    part_b = choose(part_b, exchange(send_b, 2, n), 1)
    got_a = exchange(pick(part_a, 1 - y), 2, n)
    got_b = exchange(pick(part_b, 1 - x), 1, n)
    piece = jnp.concatenate(
        [choose(pick(part_a, y), got_a, 1), choose(pick(part_b, x), got_b, 0)], axis=1
    )
    piece = before(piece)
    last = n.bit_length() - 2
    for bit in range(2, last):
        piece = choose(piece, exchange(piece, 1 << bit, n), bit)
    near = (me >> 2) & 1
    own = jnp.where(near == 0, piece[:, : half // 2], piece[:, half // 2 :])
    own = choose(own, exchange(own, 1 << last, n), last)
    piece = between(jnp.concatenate([own, exchange(own, 4, n)], axis=1))
    got_x, got_y = exchange(piece, 1, n), after(exchange(piece, 2, n))
    across_a = exchange(got_y[:, : half // 2], 1, n)
    across_b = exchange(got_x[:, half // 2 :], 2, n)
    pieces = [piece, got_x, got_y, across_a, across_b]
    mine, other_sums = project(
        pieces, key_weight, value_weight, jnp.stack([place, is_long, near]), positions
    )
    return (mine + swap(other_sums)).astype(jnp.bfloat16)


def text_of_clip(embed, key_weight, value_weight, encoder):
    kept = jnp.where(lax.axis_index("seq") == encoder, embed, 0).astype(embed.dtype)
    prompt = lax.psum(kept, "seq")
    weight = lax.all_gather(
        jnp.concatenate([key_weight, value_weight], axis=1), "dp", axis=0, tiled=True
    )
    return jnp.dot(prompt, weight, preferred_element_type=jnp.float32).astype(jnp.bfloat16)


def shards(
    n_dp,
    n,
    self_query,
    self_key,
    self_value,
    cross_query,
    text_embed,
    cross_key_weight,
    cross_value_weight,
    text_lengths,
    encoder_index,
):
    heads = cross_key_weight.shape[1] // HEAD
    inputs = [self_query[0], self_key[0], self_value[0], cross_query[0]]
    embed, weights = text_embed[0, 0], (cross_key_weight, cross_value_weight)
    if n_dp != 2 or n < 16 or n & (n - 1) or heads % 2:
        blocks = spread(pack(inputs, n, [(a, 0) for a in range(4)], heads * HEAD))
        text = text_of_clip(embed, *weights, encoder_index[0])
        self_out = self_attention(blocks, 0, False)
        out = cross_attention(blocks, 3, text, 0, text_lengths, self_out)
        return unpack([spread(out)])[None]

    part = heads // 2 * HEAD
    lines = spread_lines(pack(inputs, n, [(0, 0), (1, 0), (2, 0)], part))
    rest = pack(inputs, n, [(3, 0), (0, 1), (1, 1), (2, 1), (3, 1)], part)
    self_first = later = None

    def before(piece):
        nonlocal lines, self_first
        lines, piece = lax.optimization_barrier((lines, piece))
        self_first = self_attention(spread_planes(lines), 0, True)
        return piece

    def between(piece):
        nonlocal rest, later
        piece, rest = lax.optimization_barrier((piece, rest))
        later = spread(rest)
        return piece

    def after(piece):
        nonlocal self_first
        piece, self_first = lax.optimization_barrier((piece, self_first))
        return piece

    text = text_of_pair(
        embed, *weights, text_lengths[0], encoder_index[0], n, before, between, after
    )
    out = cross_attention(later, 0, text, 0, text_lengths, self_first)
    tokens = spread(out)
    later, out = lax.optimization_barrier((later, out))
    self_second = self_attention(later, 1, False)
    out = cross_attention(later, 4, text, heads // 2, text_lengths, self_second)
    tokens, out = lax.optimization_barrier((tokens, out))
    return unpack([tokens, spread(out)])[None]


def solution(mesh):
    placed = (
        P("dp", "seq", None),
        P("dp", "seq", None),
        P("dp", "seq", None),
        P("dp", "seq", None),
        P("dp", "seq", None, None),
        P("dp", "seq"),
        P("dp", "seq"),
        P("dp"),
        P("dp"),
    )
    return jax.shard_map(
        functools.partial(shards, mesh.shape["dp"], mesh.shape["seq"]),
        mesh=mesh,
        in_specs=placed,
        out_specs=P("dp", "seq", None),
        check_vma=False,
    )
```

```python
import functools
import math

import jax
import jax.numpy as jnp
from jax import lax
from jax.experimental import pallas as pl
from jax.experimental.pallas import tpu as pltpu
from jax.sharding import PartitionSpec as P

HEAD = 128
QUAD = 4
LOG2E = math.log2(math.e)


def params(mebibytes=48):
    return pltpu.CompilerParams(vmem_limit_bytes=mebibytes * 1024 * 1024)


def pack(arrays, n, items, part):
    rows, columns = arrays[0].shape
    width = columns // n
    per = max(1, n // 4)
    used = sorted({a for a, _ in items})

    def body(*refs):
        for i, (a, g) in enumerate(items):
            for j in range(per):
                start = j * width + g * part
                refs[-1][j, i] = refs[used.index(a)][:, start : start + part]

    return pl.pallas_call(
        body,
        grid=(n // per,),
        in_specs=[pl.BlockSpec((rows, per * width), lambda i: (0, i))] * len(used),
        out_specs=pl.BlockSpec((per, len(items), rows, part), lambda i: (i, 0, 0, 0)),
        out_shape=jax.ShapeDtypeStruct((n, len(items), rows, part), arrays[0].dtype),
        compiler_params=params(60),
        name="pack",
    )(*[arrays[a] for a in used])


def unpack(parts):
    groups = len(parts)
    n, rows, part = parts[0].shape
    width = part * groups
    per = max(1, n // 4)

    def body(*refs):
        for g in range(groups):
            for j in range(per):
                start = j * width + g * part
                refs[groups][:, start : start + part] = refs[g][j]

    return pl.pallas_call(
        body,
        grid=(n // per,),
        in_specs=[pl.BlockSpec((per, rows, part), lambda i: (i, 0, 0))] * groups,
        out_specs=pl.BlockSpec((rows, per * width), lambda i: (0, i)),
        out_shape=jax.ShapeDtypeStruct((rows, n * width), parts[0].dtype),
        compiler_params=params(),
        name="unpack",
    )(*parts)


def result_blocks(n, step, rows, turned):
    if turned:
        lines = n // QUAD
        return (lines, QUAD, rows), pl.BlockSpec(
            (lines, 1, rows, HEAD), lambda h, i, *_: (0, i, 0, h)
        )
    return (n // step, step, rows), pl.BlockSpec(
        (1, step, rows, HEAD), lambda h, i, *_: (i, 0, 0, h)
    )


def self_attention(blocks, first, turned):
    n, _, rows, width = blocks.shape
    heads = width // HEAD
    tokens = n * rows
    per = max(1, min(n, 256 // rows))
    step = n // QUAD if turned else 2 * per
    factor = LOG2E / HEAD**0.5
    shape, out_block = result_blocks(n, step, rows, turned)

    def body(q_ref, k_ref, v_ref, out_ref, values):
        @pl.when(pl.program_id(1) == 0)
        def _():
            values[:, :HEAD] = v_ref[:, 0].reshape(tokens, HEAD)
            values[:, HEAD:] = jnp.ones((tokens, HEAD), jnp.bfloat16)

        keys = k_ref[:, 0].reshape(tokens, HEAD)
        outs = []
        for part in range(step // per):
            q = q_ref[part * per : (part + 1) * per, 0].reshape(per * rows, HEAD)
            scores = lax.dot_general(
                q, keys, (((1,), (1,)), ((), ())), preferred_element_type=jnp.float32
            )
            top = jnp.max(scores, axis=1, keepdims=True)
            probs = jnp.exp2((scores - top) * factor).astype(jnp.bfloat16)
            total = jnp.dot(probs, values[...], preferred_element_type=jnp.float32)
            outs.append((total[:, :HEAD] / total[:, HEAD:]).astype(jnp.bfloat16))
        out_ref[...] = jnp.concatenate(outs).reshape(out_ref.shape)

    return pl.pallas_call(
        body,
        grid=(heads, n // step),
        in_specs=[
            pl.BlockSpec((step, 1, rows, HEAD), lambda h, i: (i, first, 0, h)),
            pl.BlockSpec((n, 1, rows, HEAD), lambda h, i: (0, first + 1, 0, h)),
            pl.BlockSpec((n, 1, rows, HEAD), lambda h, i: (0, first + 2, 0, h)),
        ],
        out_specs=out_block,
        out_shape=jax.ShapeDtypeStruct((*shape, width), jnp.bfloat16),
        scratch_shapes=[pltpu.VMEM((tokens, 2 * HEAD), jnp.bfloat16)],
        compiler_params=params(),
        cost_estimate=pl.CostEstimate(
            flops=16 * heads * tokens * tokens * HEAD,
            bytes_accessed=2 * 4 * tokens * width,
            transcendentals=heads * tokens * tokens,
        ),
        name="self_attention",
    )(blocks, blocks, blocks).reshape(n, rows, width)


def cross_attention(blocks, item, text, head, length, self_out, turned):
    n, _, rows, width = blocks.shape
    heads = width // HEAD
    positions = text.shape[0]
    values_at = text.shape[1] // HEAD // 2 + head
    step = n // QUAD if turned else max(1, min(n, 512 // rows))
    factor = LOG2E / HEAD**0.5
    shape, out_block = result_blocks(n, step, rows, turned)

    def body(length_ref, q_ref, k_ref, v_ref, self_ref, out_ref, values):
        @pl.when(pl.program_id(1) == 0)
        def _():
            values[:, :HEAD] = v_ref[...]
            values[:, HEAD:] = jnp.ones((positions, HEAD), jnp.bfloat16)

        q = q_ref[:, 0].reshape(step * rows, HEAD)
        scores = lax.dot_general(
            q, k_ref[...], (((1,), (1,)), ((), ())), preferred_element_type=jnp.float32
        )
        place = lax.broadcasted_iota(jnp.int32, (1, positions), 1)
        scores = jnp.where(place < length_ref[0], scores, -1e30)
        top = jnp.max(scores, axis=1, keepdims=True)
        probs = jnp.exp2((scores - top) * factor).astype(jnp.bfloat16)
        total = jnp.dot(probs, values[...], preferred_element_type=jnp.float32)
        out = (total[:, :HEAD] / total[:, HEAD:]).astype(jnp.bfloat16).astype(jnp.float32)
        out = out.reshape(self_ref.shape) + self_ref[...].astype(jnp.float32)
        out_ref[...] = out.astype(jnp.bfloat16)

    return pl.pallas_call(
        body,
        grid_spec=pltpu.PrefetchScalarGridSpec(
            num_scalar_prefetch=1,
            grid=(heads, n // step),
            in_specs=[
                pl.BlockSpec((step, 1, rows, HEAD), lambda h, i, _: (i, item, 0, h)),
                pl.BlockSpec((positions, HEAD), lambda h, i, _: (0, head + h)),
                pl.BlockSpec((positions, HEAD), lambda h, i, _: (0, values_at + h)),
                out_block,
            ],
            out_specs=out_block,
            scratch_shapes=[pltpu.VMEM((positions, 2 * HEAD), jnp.bfloat16)],
        ),
        out_shape=jax.ShapeDtypeStruct((*shape, width), jnp.bfloat16),
        compiler_params=params(),
        cost_estimate=pl.CostEstimate(
            flops=32 * heads * n * rows * positions * HEAD,
            bytes_accessed=2 * 3 * n * rows * width,
            transcendentals=heads * n * rows * positions,
        ),
        name="cross_attention",
    )(length, blocks, text, text, self_out.reshape(*shape, width)).reshape(n, rows, width)


def spread(blocks, groups=None):
    flat = blocks.reshape(blocks.shape[0], -1, blocks.shape[-1])
    return lax.all_to_all(
        flat, "seq", split_axis=0, concat_axis=0, tiled=True, axis_index_groups=groups
    ).reshape(blocks.shape)


def spread_lines(blocks):
    n = blocks.shape[0]
    return spread(blocks, [[q + QUAD * z for z in range(n // QUAD)] for q in range(QUAD)])


def spread_planes(blocks):
    n = blocks.shape[0]
    shape = blocks.shape[1:]
    turned = blocks.reshape(n // QUAD, QUAD, *shape).swapaxes(0, 1).reshape(n, *shape)
    return spread(turned, [[QUAD * z + q for q in range(QUAD)] for z in range(n // QUAD)])


def exchange(value, apart, n):
    return lax.ppermute(value, "seq", [(i, i ^ apart) for i in range(n)])


def pick(value, index):
    return lax.dynamic_index_in_dim(value, index, 0, keepdims=False)


def swap(value):
    return lax.ppermute(value, "dp", [(0, 1), (1, 0)])


def quarters(embed, other, where):
    positions, columns = embed.shape
    rows_long, rows_short = positions // 4, positions // 32
    rows = rows_long + rows_short
    half, part = columns // 2, columns // 4

    def body(where_ref, own_ref, other_ref, send_a, keep_a, send_b, keep_b):
        x, y = where_ref[2] & 1, where_ref[2] >> 1

        def fill(long_ref, short_ref):
            for i in range(2):
                for ref, place, first in (
                    (send_a, 2 * i + 1 - x, 0),
                    (keep_a, 2 * i + x, 0),
                    (send_b, 2 * (1 - y) + i, part),
                    (keep_b, 2 * y + i, part),
                ):
                    across = slice(first, first + part)
                    at_long = pl.ds(pl.multiple_of(place * rows_long, rows_long), rows_long)
                    at_short = pl.ds(pl.multiple_of(place * rows_short, rows_short), rows_short)
                    ref[i, :rows_long] = long_ref[at_long, across]
                    ref[i, rows_long:] = short_ref[at_short, across]

        @pl.when(where_ref[1] == 1)
        def _():
            fill(own_ref, other_ref)

        @pl.when(where_ref[1] == 0)
        def _():
            fill(other_ref, own_ref)

    return pl.pallas_call(
        body,
        grid_spec=pltpu.PrefetchScalarGridSpec(
            num_scalar_prefetch=1,
            grid=(1,),
            in_specs=[pl.BlockSpec((positions, half), lambda i, w: (0, w[0]))] * 2,
            out_specs=[pl.BlockSpec((2, rows, part), lambda i, w: (0, 0, 0))] * 4,
        ),
        out_shape=[jax.ShapeDtypeStruct((2, rows, part), embed.dtype)] * 4,
        compiler_params=params(),
        name="quarters",
    )(where, embed, other)


def project(pieces, key_weight, value_weight, where, positions):
    rows, half = pieces[0].shape
    columns, width = key_weight.shape
    rows_long, rows_short = positions // 4, positions // 32

    def body(where_ref, *refs):
        piece_refs, (key_ref, value_ref, mine_ref, sent_ref) = refs[:10], refs[10:]
        whole_pieces = [ref[...] for ref in piece_refs]
        lefts, rights = [
            side[:3] + [jnp.concatenate(side[3:], axis=1)]
            for side in (whole_pieces[:5], whole_pieces[5:])
        ]

        def fill(long_ref, short_ref):
            short_ref[4 * rows_short :] = jnp.zeros(
                (positions - 4 * rows_short, 2 * width), jnp.float32
            )
            near = where_ref[2]
            first = pl.ds(pl.multiple_of(near * half, half), half)
            second = pl.ds(pl.multiple_of((1 - near) * half, half), half)
            for i, (left, right) in enumerate(zip(lefts, rights)):
                place = where_ref[0] ^ i
                at_long = pl.ds(pl.multiple_of(place * rows_long, rows_long), rows_long)
                at_short = pl.ds(pl.multiple_of(place * rows_short, rows_short), rows_short)
                for j, ref in enumerate((key_ref, value_ref)):
                    sums = jnp.dot(left, ref[first], preferred_element_type=jnp.float32)
                    sums += jnp.dot(right, ref[second], preferred_element_type=jnp.float32)
                    across = slice(j * width, (j + 1) * width)
                    long_ref[at_long, across] = sums[:rows_long]
                    short_ref[at_short, across] = sums[rows_long:]

        @pl.when(where_ref[1] == 1)
        def _():
            fill(mine_ref, sent_ref)

        @pl.when(where_ref[1] == 0)
        def _():
            fill(sent_ref, mine_ref)

    def whole(*shape):
        return pl.BlockSpec(shape, lambda i, w: (0, 0))

    return pl.pallas_call(
        body,
        grid_spec=pltpu.PrefetchScalarGridSpec(
            num_scalar_prefetch=1,
            grid=(1,),
            in_specs=([whole(rows, half)] * 3 + [whole(rows, half // 2)] * 2) * 2
            + [whole(columns, width)] * 2,
            out_specs=[whole(positions, 2 * width)] * 2,
        ),
        out_shape=[jax.ShapeDtypeStruct((positions, 2 * width), jnp.float32)] * 2,
        compiler_params=params(),
        cost_estimate=pl.CostEstimate(
            flops=18000000000, bytes_accessed=8 * 1024 * 1024, transcendentals=0
        ),
        name="project",
    )(where, *pieces, key_weight, value_weight)


def text_of_pair(embed, key_weight, value_weight, length, encoder, n, between, after):
    positions, columns = embed.shape
    core = lax.axis_index("dp")
    me = lax.axis_index("seq")
    half = columns // 2
    other = swap(embed)
    other_facts = swap(jnp.stack([length, encoder]))
    mine_long = length > other_facts[0]
    encoder_long = jnp.where(mine_long, encoder, other_facts[1])
    encoder_short = jnp.where(mine_long, other_facts[1], encoder)
    rows_long, rows_short = positions // 4, positions // 32
    rows = rows_long + rows_short
    place = me & 3
    is_long = mine_long.astype(jnp.int32)
    send_a, part_a, send_b, part_b = quarters(embed, other, jnp.stack([core, is_long, place]))
    on_row = lax.broadcasted_iota(jnp.int32, (rows, 1), 0)
    apart = jnp.where(on_row < rows_long, encoder_long, encoder_short) ^ me
    x, y = me & 1, (me >> 1) & 1

    def choose(own, got, bit):
        return jnp.where((apart >> bit) & 1 == 0, own, got)

    part_a = choose(part_a, exchange(send_a, 1, n), 0)
    part_b = choose(part_b, exchange(send_b, 2, n), 1)
    got_a = exchange(pick(part_a, 1 - y), 2, n)
    got_b = exchange(pick(part_b, 1 - x), 1, n)
    piece = jnp.concatenate(
        [choose(pick(part_a, y), got_a, 1), choose(pick(part_b, x), got_b, 0)], axis=1
    )
    last = n.bit_length() - 2
    for bit in range(2, last):
        piece = choose(piece, exchange(piece, 1 << bit, n), bit)
    near = (me >> 2) & 1
    own = jnp.where(near == 0, piece[:, : half // 2], piece[:, half // 2 :])
    own = between(choose(own, exchange(own, 1 << last, n), last))
    far, own_x, own_y = exchange(own, 4, n), exchange(own, 1, n), after(exchange(own, 2, n))
    pieces = []
    for here, at_x, at_y in (
        (own, own_x, own_y),
        (far, exchange(far, 1, n), exchange(far, 2, n)),
    ):
        across_a = exchange(at_y[:, : half // 4], 1, n)
        across_b = exchange(at_x[:, half // 4 :], 2, n)
        pieces += [here, at_x, at_y, across_a, across_b]
    mine, other_sums = project(
        pieces, key_weight, value_weight, jnp.stack([place, is_long, near]), positions
    )
    return (mine + swap(other_sums)).astype(jnp.bfloat16)


def text_of_clip(embed, key_weight, value_weight, encoder):
    kept = jnp.where(lax.axis_index("seq") == encoder, embed, 0).astype(embed.dtype)
    prompt = lax.psum(kept, "seq")
    weight = lax.all_gather(
        jnp.concatenate([key_weight, value_weight], axis=1), "dp", axis=0, tiled=True
    )
    return jnp.dot(prompt, weight, preferred_element_type=jnp.float32).astype(jnp.bfloat16)


def shards(
    n_dp,
    n,
    self_query,
    self_key,
    self_value,
    cross_query,
    text_embed,
    cross_key_weight,
    cross_value_weight,
    text_lengths,
    encoder_index,
):
    heads = cross_key_weight.shape[1] // HEAD
    inputs = [self_query[0], self_key[0], self_value[0], cross_query[0]]
    embed, weights = text_embed[0, 0], (cross_key_weight, cross_value_weight)
    if n_dp != 2 or n < 16 or n & (n - 1) or heads % 2:
        blocks = spread(pack(inputs, n, [(a, 0) for a in range(4)], heads * HEAD))
        text = text_of_clip(embed, *weights, encoder_index[0])
        self_out = self_attention(blocks, 0, False)
        out = cross_attention(blocks, 3, text, 0, text_lengths, self_out, False)
        return unpack([spread(out)])[None]

    part = heads // 2 * HEAD
    lines = spread_lines(pack(inputs, n, [(a, 0) for a in range(4)], part))
    rest = pack(inputs, n, [(a, 1) for a in range(4)], part)
    earlier = spread_planes(lines)
    self_first = later = None

    def between(piece):
        nonlocal rest, earlier, self_first, later
        piece, rest, earlier = lax.optimization_barrier((piece, rest, earlier))
        self_first = self_attention(earlier, 0, True)
        later = spread(rest)
        return piece

    def after(piece):
        nonlocal self_first
        piece, self_first = lax.optimization_barrier((piece, self_first))
        return piece

    text = text_of_pair(
        embed, *weights, text_lengths[0], encoder_index[0], n, between, after
    )
    out = cross_attention(earlier, 3, text, 0, text_lengths, self_first, True)
    later, out = lax.optimization_barrier((later, out))
    tokens = spread(out)
    self_second = self_attention(later, 0, False)
    out = cross_attention(later, 3, text, heads // 2, text_lengths, self_second, False)
    tokens, out = lax.optimization_barrier((tokens, out))
    return unpack([tokens, spread(out)])[None]


def solution(mesh):
    placed = (
        P("dp", "seq", None),
        P("dp", "seq", None),
        P("dp", "seq", None),
        P("dp", "seq", None),
        P("dp", "seq", None, None),
        P("dp", "seq"),
        P("dp", "seq"),
        P("dp"),
        P("dp"),
    )
    return jax.shard_map(
        functools.partial(shards, mesh.shape["dp"], mesh.shape["seq"]),
        mesh=mesh,
        in_specs=placed,
        out_specs=P("dp", "seq", None),
        check_vma=False,
    )
```

```python
import functools
import math

import jax
import jax.numpy as jnp
from jax import lax
from jax.experimental import pallas as pl
from jax.experimental.pallas import tpu as pltpu
from jax.sharding import PartitionSpec as P

HEAD = 128
QUAD = 4
LOG2E = math.log2(math.e)


def params(mebibytes=48):
    return pltpu.CompilerParams(vmem_limit_bytes=mebibytes * 1024 * 1024)


def small():
    return pl.CostEstimate(flops=0, bytes_accessed=4 * 1024 * 1024, transcendentals=0)


def pack(arrays, n, items, part):
    rows, columns = arrays[0].shape
    width = columns // n
    per = max(1, n // 4)
    used = sorted({a for a, _ in items})

    def body(*refs):
        for i, (a, g) in enumerate(items):
            for j in range(per):
                start = j * width + g * part
                refs[-1][j, i] = refs[used.index(a)][:, start : start + part]

    return pl.pallas_call(
        body,
        grid=(n // per,),
        in_specs=[pl.BlockSpec((rows, per * width), lambda i: (0, i))] * len(used),
        out_specs=pl.BlockSpec((per, len(items), rows, part), lambda i: (i, 0, 0, 0)),
        out_shape=jax.ShapeDtypeStruct((n, len(items), rows, part), arrays[0].dtype),
        compiler_params=params(60),
        cost_estimate=small(),
        name="pack",
    )(*[arrays[a] for a in used])


def unpack(parts):
    groups = len(parts)
    n, rows, part = parts[0].shape
    width = part * groups
    per = max(1, n // 4)

    def body(*refs):
        for g in range(groups):
            for j in range(per):
                start = j * width + g * part
                refs[groups][:, start : start + part] = refs[g][j]

    return pl.pallas_call(
        body,
        grid=(n // per,),
        in_specs=[pl.BlockSpec((per, rows, part), lambda i: (i, 0, 0))] * groups,
        out_specs=pl.BlockSpec((rows, per * width), lambda i: (0, i)),
        out_shape=jax.ShapeDtypeStruct((rows, n * width), parts[0].dtype),
        compiler_params=params(),
        cost_estimate=small(),
        name="unpack",
    )(*parts)


def self_attention(blocks, first, place=None):
    n, _, rows, width = blocks.shape
    heads = width // HEAD
    tokens = n * rows
    per = max(1, min(n, 256 // rows))
    factor = LOG2E / HEAD**0.5
    if place is None:
        step, place = 2 * per, jnp.zeros(1, jnp.int32)
        shape = (n // step, step, rows)
        out_block = pl.BlockSpec((1, step, rows, HEAD), lambda h, i, _: (i, 0, 0, h))
    else:
        step, place = n // QUAD, place.reshape(1)
        shape = (step, QUAD, rows)
        out_block = pl.BlockSpec((step, 1, rows, HEAD), lambda h, i, p: (0, i ^ p[0], 0, h))

    def body(_, q_ref, k_ref, v_ref, out_ref, values):
        @pl.when(pl.program_id(1) == 0)
        def _():
            values[:, :HEAD] = v_ref[:, 0].reshape(tokens, HEAD)
            values[:, HEAD:] = jnp.ones((tokens, HEAD), jnp.bfloat16)

        keys = k_ref[:, 0].reshape(tokens, HEAD)
        outs = []
        for part in range(step // per):
            q = q_ref[part * per : (part + 1) * per, 0].reshape(per * rows, HEAD)
            scores = lax.dot_general(
                q, keys, (((1,), (1,)), ((), ())), preferred_element_type=jnp.float32
            )
            top = jnp.max(scores, axis=1, keepdims=True)
            probs = jnp.exp2((scores - top) * factor).astype(jnp.bfloat16)
            total = jnp.dot(probs, values[...], preferred_element_type=jnp.float32)
            outs.append((total[:, :HEAD] / total[:, HEAD:]).astype(jnp.bfloat16))
        out_ref[...] = jnp.concatenate(outs).reshape(out_ref.shape)

    return pl.pallas_call(
        body,
        grid_spec=pltpu.PrefetchScalarGridSpec(
            num_scalar_prefetch=1,
            grid=(heads, n // step),
            in_specs=[
                pl.BlockSpec((step, 1, rows, HEAD), lambda h, i, _: (i, first, 0, h)),
                pl.BlockSpec((n, 1, rows, HEAD), lambda h, i, _: (0, first + 1, 0, h)),
                pl.BlockSpec((n, 1, rows, HEAD), lambda h, i, _: (0, first + 2, 0, h)),
            ],
            out_specs=out_block,
            scratch_shapes=[pltpu.VMEM((tokens, 2 * HEAD), jnp.bfloat16)],
        ),
        out_shape=jax.ShapeDtypeStruct((*shape, width), jnp.bfloat16),
        compiler_params=params(),
        cost_estimate=pl.CostEstimate(
            flops=16 * heads * tokens * tokens * HEAD,
            bytes_accessed=2 * 4 * tokens * width,
            transcendentals=heads * tokens * tokens,
        ),
        name="self_attention",
    )(place, blocks, blocks, blocks).reshape(n, rows, width)


def cross_attention(blocks, item, text, head, length, self_out, place=None):
    n, _, rows, width = blocks.shape
    heads = width // HEAD
    positions = text.shape[0]
    values_at = text.shape[1] // HEAD // 2 + head
    step = max(1, min(n, 512 // rows))
    factor = LOG2E / HEAD**0.5
    if place is None:
        place = jnp.zeros(1, jnp.int32)
        shape = (n // step, step, rows)
        out_block = pl.BlockSpec((1, step, rows, HEAD), lambda h, i, *_: (i, 0, 0, h))
    else:
        step, place = n // QUAD, place.reshape(1)
        shape = (step, QUAD, rows)
        out_block = pl.BlockSpec((step, 1, rows, HEAD), lambda h, i, _, p: (0, i ^ p[0], 0, h))

    def body(length_ref, _, q_ref, k_ref, v_ref, self_ref, out_ref, values):
        @pl.when(pl.program_id(1) == 0)
        def _():
            values[:, :HEAD] = v_ref[...]
            values[:, HEAD:] = jnp.ones((positions, HEAD), jnp.bfloat16)

        q = q_ref[:, 0].reshape(step * rows, HEAD)
        scores = lax.dot_general(
            q, k_ref[...], (((1,), (1,)), ((), ())), preferred_element_type=jnp.float32
        )
        place = lax.broadcasted_iota(jnp.int32, (1, positions), 1)
        scores = jnp.where(place < length_ref[0], scores, -1e30)
        top = jnp.max(scores, axis=1, keepdims=True)
        probs = jnp.exp2((scores - top) * factor).astype(jnp.bfloat16)
        total = jnp.dot(probs, values[...], preferred_element_type=jnp.float32)
        out = (total[:, :HEAD] / total[:, HEAD:]).astype(jnp.bfloat16).astype(jnp.float32)
        out = out.reshape(self_ref.shape) + self_ref[...].astype(jnp.float32)
        out_ref[...] = out.astype(jnp.bfloat16)

    return pl.pallas_call(
        body,
        grid_spec=pltpu.PrefetchScalarGridSpec(
            num_scalar_prefetch=2,
            grid=(heads, n // step),
            in_specs=[
                pl.BlockSpec((step, 1, rows, HEAD), lambda h, i, *_: (i, item, 0, h)),
                pl.BlockSpec((positions, HEAD), lambda h, i, *_: (0, head + h)),
                pl.BlockSpec((positions, HEAD), lambda h, i, *_: (0, values_at + h)),
                out_block,
            ],
            out_specs=out_block,
            scratch_shapes=[pltpu.VMEM((positions, 2 * HEAD), jnp.bfloat16)],
        ),
        out_shape=jax.ShapeDtypeStruct((*shape, width), jnp.bfloat16),
        compiler_params=params(),
        cost_estimate=pl.CostEstimate(
            flops=32 * heads * n * rows * positions * HEAD,
            bytes_accessed=2 * 3 * n * rows * width,
            transcendentals=heads * n * rows * positions,
        ),
        name="cross_attention",
    )(length, place, blocks, text, text, self_out.reshape(*shape, width)).reshape(n, rows, width)


def spread(blocks, groups=None):
    flat = blocks.reshape(blocks.shape[0], -1, blocks.shape[-1])
    return lax.all_to_all(
        flat, "seq", split_axis=0, concat_axis=0, tiled=True, axis_index_groups=groups
    ).reshape(blocks.shape)


def spread_lines(blocks):
    n = blocks.shape[0]
    return spread(blocks, [[q + QUAD * z for z in range(n // QUAD)] for q in range(QUAD)])


def join(parts):
    count = len(parts)
    planes, *rest = parts[0].shape

    def body(*refs):
        for i in range(count):
            refs[count][i] = refs[i][...]

    return pl.pallas_call(
        body,
        grid=(planes,),
        in_specs=[pl.BlockSpec((1, *rest), lambda i: (i, 0, 0, 0))] * count,
        out_specs=pl.BlockSpec((count, 1, *rest), lambda i: (0, i, 0, 0, 0)),
        out_shape=jax.ShapeDtypeStruct((count, planes, *rest), parts[0].dtype),
        compiler_params=params(),
        cost_estimate=pl.CostEstimate(
            flops=10000000000, bytes_accessed=4 * 1024 * 1024, transcendentals=0
        ),
        name="join",
    )(*parts).reshape(count * planes, *rest)


def spread_planes(blocks, place):
    n = blocks.shape[0]
    lines = blocks.reshape(n // QUAD, QUAD, *blocks.shape[1:])
    sent = [lax.dynamic_index_in_dim(lines, place ^ r, 1, keepdims=False) for r in range(QUAD)]
    return join([sent[0]] + [exchange(sent[r], r, n) for r in range(1, QUAD)])


def exchange(value, apart, n):
    return lax.ppermute(value, "seq", [(i, i ^ apart) for i in range(n)])


def pick(value, index):
    return lax.dynamic_index_in_dim(value, index, 0, keepdims=False)


def swap(value):
    return lax.ppermute(value, "dp", [(0, 1), (1, 0)])


def quarters(embed, other, where):
    positions, columns = embed.shape
    rows_long, rows_short = positions // 4, positions // 32
    rows = rows_long + rows_short
    half, part = columns // 2, columns // 4

    def body(where_ref, own_ref, other_ref, send_a, keep_a, send_b, keep_b):
        x, y = where_ref[2] & 1, where_ref[2] >> 1

        def fill(long_ref, short_ref):
            for i in range(2):
                for ref, place, first in (
                    (send_a, 2 * i + 1 - x, 0),
                    (keep_a, 2 * i + x, 0),
                    (send_b, 2 * (1 - y) + i, part),
                    (keep_b, 2 * y + i, part),
                ):
                    across = slice(first, first + part)
                    at_long = pl.ds(pl.multiple_of(place * rows_long, rows_long), rows_long)
                    at_short = pl.ds(pl.multiple_of(place * rows_short, rows_short), rows_short)
                    ref[i, :rows_long] = long_ref[at_long, across]
                    ref[i, rows_long:] = short_ref[at_short, across]

        @pl.when(where_ref[1] == 1)
        def _():
            fill(own_ref, other_ref)

        @pl.when(where_ref[1] == 0)
        def _():
            fill(other_ref, own_ref)

    return pl.pallas_call(
        body,
        grid_spec=pltpu.PrefetchScalarGridSpec(
            num_scalar_prefetch=1,
            grid=(1,),
            in_specs=[pl.BlockSpec((positions, half), lambda i, w: (0, w[0]))] * 2,
            out_specs=[pl.BlockSpec((2, rows, part), lambda i, w: (0, 0, 0))] * 4,
        ),
        out_shape=[jax.ShapeDtypeStruct((2, rows, part), embed.dtype)] * 4,
        compiler_params=params(),
        cost_estimate=small(),
        name="quarters",
    )(where, embed, other)


def project(pieces, key_weight, value_weight, where, positions):
    rows, half = pieces[0].shape
    columns, width = key_weight.shape
    rows_long, rows_short = positions // 4, positions // 32

    def body(where_ref, *refs):
        piece_refs, (key_ref, value_ref, mine_ref, sent_ref) = refs[:10], refs[10:]
        whole_pieces = [ref[...] for ref in piece_refs]
        lefts, rights = [
            side[:3] + [jnp.concatenate(side[3:], axis=1)]
            for side in (whole_pieces[:5], whole_pieces[5:])
        ]

        def fill(long_ref, short_ref):
            short_ref[4 * rows_short :] = jnp.zeros(
                (positions - 4 * rows_short, 2 * width), jnp.float32
            )
            near = where_ref[2]
            first = pl.ds(pl.multiple_of(near * half, half), half)
            second = pl.ds(pl.multiple_of((1 - near) * half, half), half)
            for i, (left, right) in enumerate(zip(lefts, rights)):
                place = where_ref[0] ^ i
                at_long = pl.ds(pl.multiple_of(place * rows_long, rows_long), rows_long)
                at_short = pl.ds(pl.multiple_of(place * rows_short, rows_short), rows_short)
                for j, ref in enumerate((key_ref, value_ref)):
                    sums = jnp.dot(left, ref[first], preferred_element_type=jnp.float32)
                    sums += jnp.dot(right, ref[second], preferred_element_type=jnp.float32)
                    across = slice(j * width, (j + 1) * width)
                    long_ref[at_long, across] = sums[:rows_long]
                    short_ref[at_short, across] = sums[rows_long:]

        @pl.when(where_ref[1] == 1)
        def _():
            fill(mine_ref, sent_ref)

        @pl.when(where_ref[1] == 0)
        def _():
            fill(sent_ref, mine_ref)

    def whole(*shape):
        return pl.BlockSpec(shape, lambda i, w: (0, 0))

    return pl.pallas_call(
        body,
        grid_spec=pltpu.PrefetchScalarGridSpec(
            num_scalar_prefetch=1,
            grid=(1,),
            in_specs=([whole(rows, half)] * 3 + [whole(rows, half // 2)] * 2) * 2
            + [whole(columns, width)] * 2,
            out_specs=[whole(positions, 2 * width)] * 2,
        ),
        out_shape=[jax.ShapeDtypeStruct((positions, 2 * width), jnp.float32)] * 2,
        compiler_params=params(),
        cost_estimate=pl.CostEstimate(
            flops=7000000000, bytes_accessed=8 * 1024 * 1024, transcendentals=0
        ),
        name="project",
    )(where, *pieces, key_weight, value_weight)


def text_of_pair(embed, key_weight, value_weight, length, encoder, n, before, between, after):
    positions, columns = embed.shape
    core = lax.axis_index("dp")
    me = lax.axis_index("seq")
    half = columns // 2
    other = swap(embed)
    other_facts = swap(jnp.stack([length, encoder]))
    mine_long = length > other_facts[0]
    encoder_long = jnp.where(mine_long, encoder, other_facts[1])
    encoder_short = jnp.where(mine_long, other_facts[1], encoder)
    rows_long, rows_short = positions // 4, positions // 32
    rows = rows_long + rows_short
    place = me & 3
    is_long = mine_long.astype(jnp.int32)
    send_a, part_a, send_b, part_b = quarters(embed, other, jnp.stack([core, is_long, place]))
    on_row = lax.broadcasted_iota(jnp.int32, (rows, 1), 0)
    apart = jnp.where(on_row < rows_long, encoder_long, encoder_short) ^ me
    x, y = me & 1, (me >> 1) & 1

    def choose(own, got, bit):
        return jnp.where((apart >> bit) & 1 == 0, own, got)

    part_a = choose(part_a, exchange(send_a, 1, n), 0)
    part_b = choose(part_b, exchange(send_b, 2, n), 1)
    got_a = exchange(pick(part_a, 1 - y), 2, n)
    got_b = exchange(pick(part_b, 1 - x), 1, n)
    piece = jnp.concatenate(
        [choose(pick(part_a, y), got_a, 1), choose(pick(part_b, x), got_b, 0)], axis=1
    )
    last = n.bit_length() - 2
    for bit in range(2, last):
        piece = choose(piece, exchange(piece, 1 << bit, n), bit)
    near = (me >> 2) & 1
    own = jnp.where(near == 0, piece[:, : half // 2], piece[:, half // 2 :])
    own = before(own)
    own = between(choose(own, exchange(own, 1 << last, n), last))
    far, own_x, own_y = exchange(own, 4, n), exchange(own, 1, n), exchange(own, 2, n)
    pieces = []
    for here, at_x, at_y in (
        (own, own_x, own_y),
        (far, exchange(far, 1, n), after(exchange(far, 2, n))),
    ):
        across_a = exchange(at_y[:, : half // 4], 1, n)
        across_b = exchange(at_x[:, half // 4 :], 2, n)
        pieces += [here, at_x, at_y, across_a, across_b]
    mine, other_sums = project(
        pieces, key_weight, value_weight, jnp.stack([place, is_long, near]), positions
    )
    return (mine + swap(other_sums)).astype(jnp.bfloat16)


def text_of_clip(embed, key_weight, value_weight, encoder):
    kept = jnp.where(lax.axis_index("seq") == encoder, embed, 0).astype(embed.dtype)
    prompt = lax.psum(kept, "seq")
    weight = lax.all_gather(
        jnp.concatenate([key_weight, value_weight], axis=1), "dp", axis=0, tiled=True
    )
    return jnp.dot(prompt, weight, preferred_element_type=jnp.float32).astype(jnp.bfloat16)


def shards(
    n_dp,
    n,
    self_query,
    self_key,
    self_value,
    cross_query,
    text_embed,
    cross_key_weight,
    cross_value_weight,
    text_lengths,
    encoder_index,
):
    heads = cross_key_weight.shape[1] // HEAD
    inputs = [self_query[0], self_key[0], self_value[0], cross_query[0]]
    embed, weights = text_embed[0, 0], (cross_key_weight, cross_value_weight)
    if n_dp != 2 or n < 16 or n & (n - 1) or heads % 2:
        blocks = spread(pack(inputs, n, [(a, 0) for a in range(4)], heads * HEAD))
        text = text_of_clip(embed, *weights, encoder_index[0])
        self_out = self_attention(blocks, 0)
        out = cross_attention(blocks, 3, text, 0, text_lengths, self_out)
        return unpack([spread(out)])[None]

    part = heads // 2 * HEAD
    place = lax.axis_index("seq") & (QUAD - 1)
    lines = spread_lines(pack(inputs, n, [(a, 0) for a in range(4)], part))
    cross_second = pack(inputs, n, [(3, 1)], part)
    lines, cross_second = lax.optimization_barrier((lines, cross_second))
    cross_second = spread(cross_second)
    earlier = spread_planes(lines[:, :3], place)
    cross_first = spread_planes(lines[:, 3:], place)
    rest = pack(inputs, n, [(a, 1) for a in range(3)], part)
    self_first = later = None

    def before(piece):
        nonlocal cross_second
        piece, cross_second = lax.optimization_barrier((piece, cross_second))
        return piece

    def between(piece):
        nonlocal rest, earlier, self_first, later
        piece, rest, earlier = lax.optimization_barrier((piece, rest, earlier))
        self_first = self_attention(earlier, 0, place)
        later = spread(rest)
        return piece

    def after(piece):
        nonlocal self_first
        piece, self_first = lax.optimization_barrier((piece, self_first))
        return piece

    text = text_of_pair(
        embed, *weights, text_lengths[0], encoder_index[0], n, before, between, after
    )
    out = cross_attention(cross_first, 0, text, 0, text_lengths, self_first, place)
    later, out = lax.optimization_barrier((later, out))
    tokens = spread(out)
    self_second = self_attention(later, 0)
    out = cross_attention(cross_second, 0, text, heads // 2, text_lengths, self_second)
    tokens, out = lax.optimization_barrier((tokens, out))
    return unpack([tokens, spread(out)])[None]


def solution(mesh):
    placed = (
        P("dp", "seq", None),
        P("dp", "seq", None),
        P("dp", "seq", None),
        P("dp", "seq", None),
        P("dp", "seq", None, None),
        P("dp", "seq"),
        P("dp", "seq"),
        P("dp"),
        P("dp"),
    )
    return jax.shard_map(
        functools.partial(shards, mesh.shape["dp"], mesh.shape["seq"]),
        mesh=mesh,
        in_specs=placed,
        out_specs=P("dp", "seq", None),
        check_vma=False,
    )
```

```python
import functools
import math

import jax
import jax.numpy as jnp
from jax import lax
from jax.experimental import pallas as pl
from jax.experimental.pallas import tpu as pltpu
from jax.sharding import PartitionSpec as P

HEAD = 128
QUAD = 4
LOG2E = math.log2(math.e)


def params(mebibytes=48):
    return pltpu.CompilerParams(vmem_limit_bytes=mebibytes * 1024 * 1024)


def small():
    return pl.CostEstimate(flops=0, bytes_accessed=4 * 1024 * 1024, transcendentals=0)


def pack(arrays, n, items, part):
    rows, columns = arrays[0].shape
    width = columns // n
    per = max(1, n // 4)
    used = sorted({a for a, _ in items})

    def body(*refs):
        for i, (a, g) in enumerate(items):
            for j in range(per):
                start = j * width + g * part
                refs[-1][j, i] = refs[used.index(a)][:, start : start + part]

    return pl.pallas_call(
        body,
        grid=(n // per,),
        in_specs=[pl.BlockSpec((rows, per * width), lambda i: (0, i))] * len(used),
        out_specs=pl.BlockSpec((per, len(items), rows, part), lambda i: (i, 0, 0, 0)),
        out_shape=jax.ShapeDtypeStruct((n, len(items), rows, part), arrays[0].dtype),
        compiler_params=params(60),
        cost_estimate=small(),
        name="pack",
    )(*[arrays[a] for a in used])


def unpack(parts):
    groups = len(parts)
    n, rows, part = parts[0].shape
    width = part * groups
    per = max(1, n // 4)

    def body(*refs):
        for g in range(groups):
            for j in range(per):
                start = j * width + g * part
                refs[groups][:, start : start + part] = refs[g][j]

    return pl.pallas_call(
        body,
        grid=(n // per,),
        in_specs=[pl.BlockSpec((per, rows, part), lambda i: (i, 0, 0))] * groups,
        out_specs=pl.BlockSpec((rows, per * width), lambda i: (0, i)),
        out_shape=jax.ShapeDtypeStruct((rows, n * width), parts[0].dtype),
        compiler_params=params(),
        cost_estimate=small(),
        name="unpack",
    )(*parts)


def self_attention(blocks, first, place=None):
    n, _, rows, width = blocks.shape
    heads = width // HEAD
    tokens = n * rows
    per = max(1, min(n, 256 // rows))
    factor = LOG2E / HEAD**0.5
    turned = place is not None
    step = n if turned else min(n, 16)
    shape = (n // QUAD, QUAD) if turned else (n,)

    def body(place_ref, q_ref, k_ref, v_ref, out_ref, values):
        @pl.when(pl.program_id(1) == 0)
        def _():
            values[:, :HEAD] = v_ref[:, 0].reshape(tokens, HEAD)
            values[:, HEAD:] = jnp.ones((tokens, HEAD), jnp.bfloat16)

        keys = k_ref[:, 0].reshape(tokens, HEAD)
        for at in range(0, step, per):
            q = q_ref[at : at + per, 0].reshape(per * rows, HEAD)
            scores = lax.dot_general(
                q, keys, (((1,), (1,)), ((), ())), preferred_element_type=jnp.float32
            )
            top = jnp.max(scores, axis=1, keepdims=True)
            probs = jnp.exp2((scores - top) * factor).astype(jnp.bfloat16)
            total = jnp.dot(probs, values[...], preferred_element_type=jnp.float32)
            out = (total[:, :HEAD] / total[:, HEAD:]).astype(jnp.bfloat16).reshape(per, rows, HEAD)
            if turned:
                r, z = divmod(at, n // QUAD)
                out_ref[z : z + per, r ^ place_ref[0]] = out
            else:
                out_ref[at : at + per] = out

    if turned:
        out_block = pl.BlockSpec((*shape, rows, HEAD), lambda h, i, _: (0, 0, 0, h))
    else:
        out_block = pl.BlockSpec((step, rows, HEAD), lambda h, i, _: (i, 0, h))
    return pl.pallas_call(
        body,
        grid_spec=pltpu.PrefetchScalarGridSpec(
            num_scalar_prefetch=1,
            grid=(heads, n // step),
            in_specs=[
                pl.BlockSpec((step, 1, rows, HEAD), lambda h, i, _: (i, first, 0, h)),
                pl.BlockSpec((n, 1, rows, HEAD), lambda h, i, _: (0, first + 1, 0, h)),
                pl.BlockSpec((n, 1, rows, HEAD), lambda h, i, _: (0, first + 2, 0, h)),
            ],
            out_specs=out_block,
            scratch_shapes=[pltpu.VMEM((tokens, 2 * HEAD), jnp.bfloat16)],
        ),
        out_shape=jax.ShapeDtypeStruct((*shape, rows, width), jnp.bfloat16),
        compiler_params=params(),
        cost_estimate=pl.CostEstimate(
            flops=16 * heads * tokens * tokens * HEAD,
            bytes_accessed=2 * 4 * tokens * width,
            transcendentals=heads * tokens * tokens,
        ),
        name="self_attention",
    )(
        place.reshape(1) if turned else jnp.zeros(1, jnp.int32), blocks, blocks, blocks
    ).reshape(n, rows, width)


def cross_attention(blocks, item, text, head, length, self_out, place=None):
    n, _, rows, width = blocks.shape
    heads = width // HEAD
    positions = text.shape[0]
    values_at = text.shape[1] // HEAD // 2 + head
    factor = LOG2E / HEAD**0.5
    turned = place is not None
    shape = (n // QUAD, QUAD) if turned else (n,)

    def body(length_ref, place_ref, q_ref, k_ref, v_ref, self_ref, out_ref, values):
        values[:, :HEAD] = v_ref[...]
        values[:, HEAD:] = jnp.ones((positions, HEAD), jnp.bfloat16)
        valid = lax.broadcasted_iota(jnp.int32, (1, positions), 1) < length_ref[0]
        for at in range(n):
            scores = lax.dot_general(
                q_ref[at, 0],
                k_ref[...],
                (((1,), (1,)), ((), ())),
                preferred_element_type=jnp.float32,
            )
            scores = jnp.where(valid, scores, -1e30)
            top = jnp.max(scores, axis=1, keepdims=True)
            probs = jnp.exp2((scores - top) * factor).astype(jnp.bfloat16)
            total = jnp.dot(probs, values[...], preferred_element_type=jnp.float32)
            out = (total[:, :HEAD] / total[:, HEAD:]).astype(jnp.bfloat16).astype(jnp.float32)
            r, z = divmod(at, n // QUAD)
            block = (z, r ^ place_ref[0]) if turned else at
            out_ref[block] = (out + self_ref[block].astype(jnp.float32)).astype(jnp.bfloat16)

    whole = pl.BlockSpec((*shape, rows, HEAD), lambda h, *_: (0,) * len(shape) + (0, h))
    return pl.pallas_call(
        body,
        grid_spec=pltpu.PrefetchScalarGridSpec(
            num_scalar_prefetch=2,
            grid=(heads,),
            in_specs=[
                pl.BlockSpec((n, 1, rows, HEAD), lambda h, *_: (0, item, 0, h)),
                pl.BlockSpec((positions, HEAD), lambda h, *_: (0, head + h)),
                pl.BlockSpec((positions, HEAD), lambda h, *_: (0, values_at + h)),
                whole,
            ],
            out_specs=whole,
            scratch_shapes=[pltpu.VMEM((positions, 2 * HEAD), jnp.bfloat16)],
        ),
        out_shape=jax.ShapeDtypeStruct((*shape, rows, width), jnp.bfloat16),
        compiler_params=params(),
        cost_estimate=pl.CostEstimate(
            flops=32 * heads * n * rows * positions * HEAD,
            bytes_accessed=2 * 3 * n * rows * width,
            transcendentals=heads * n * rows * positions,
        ),
        name="cross_attention",
    )(
        length,
        place.reshape(1) if turned else jnp.zeros(1, jnp.int32),
        blocks,
        text,
        text,
        self_out.reshape(*shape, rows, width),
    ).reshape(n, rows, width)


def spread(blocks, groups=None):
    flat = blocks.reshape(blocks.shape[0], -1, blocks.shape[-1])
    return lax.all_to_all(
        flat, "seq", split_axis=0, concat_axis=0, tiled=True, axis_index_groups=groups
    ).reshape(blocks.shape)


def spread_lines(blocks):
    n = blocks.shape[0]
    return spread(blocks, [[q + QUAD * z for z in range(n // QUAD)] for q in range(QUAD)])


def join(parts):
    count = len(parts)
    planes, *rest = parts[0].shape

    def body(*refs):
        for i in range(count):
            refs[count][i] = refs[i][...]

    return pl.pallas_call(
        body,
        grid=(planes,),
        in_specs=[pl.BlockSpec((1, *rest), lambda i: (i, 0, 0, 0))] * count,
        out_specs=pl.BlockSpec((count, 1, *rest), lambda i: (0, i, 0, 0, 0)),
        out_shape=jax.ShapeDtypeStruct((count, planes, *rest), parts[0].dtype),
        compiler_params=params(),
        cost_estimate=pl.CostEstimate(
            flops=10000000000, bytes_accessed=4 * 1024 * 1024, transcendentals=0
        ),
        name="join",
    )(*parts).reshape(count * planes, *rest)


def spread_planes(blocks, place):
    n = blocks.shape[0]
    lines = blocks.reshape(n // QUAD, QUAD, *blocks.shape[1:])
    sent = [lax.dynamic_index_in_dim(lines, place ^ r, 1, keepdims=False) for r in range(QUAD)]
    return join([sent[0]] + [exchange(sent[r], r, n) for r in range(1, QUAD)])


def exchange(value, apart, n):
    return lax.ppermute(value, "seq", [(i, i ^ apart) for i in range(n)])


def pick(value, index):
    return lax.dynamic_index_in_dim(value, index, 0, keepdims=False)


def swap(value):
    return lax.ppermute(value, "dp", [(0, 1), (1, 0)])


def quarters(embed, other, where):
    positions, columns = embed.shape
    rows_long, rows_short = positions // 4, positions // 32
    rows = rows_long + rows_short
    half, part = columns // 2, columns // 4

    def body(where_ref, own_ref, other_ref, send_a, keep_a, send_b, keep_b):
        x, y = where_ref[2] & 1, where_ref[2] >> 1

        def fill(long_ref, short_ref):
            for i in range(2):
                for ref, place, first in (
                    (send_a, 2 * i + 1 - x, 0),
                    (keep_a, 2 * i + x, 0),
                    (send_b, 2 * (1 - y) + i, part),
                    (keep_b, 2 * y + i, part),
                ):
                    across = slice(first, first + part)
                    at_long = pl.ds(pl.multiple_of(place * rows_long, rows_long), rows_long)
                    at_short = pl.ds(pl.multiple_of(place * rows_short, rows_short), rows_short)
                    ref[i, :rows_long] = long_ref[at_long, across]
                    ref[i, rows_long:] = short_ref[at_short, across]

        @pl.when(where_ref[1] == 1)
        def _():
            fill(own_ref, other_ref)

        @pl.when(where_ref[1] == 0)
        def _():
            fill(other_ref, own_ref)

    return pl.pallas_call(
        body,
        grid_spec=pltpu.PrefetchScalarGridSpec(
            num_scalar_prefetch=1,
            grid=(1,),
            in_specs=[pl.BlockSpec((positions, half), lambda i, w: (0, w[0]))] * 2,
            out_specs=[pl.BlockSpec((2, rows, part), lambda i, w: (0, 0, 0))] * 4,
        ),
        out_shape=[jax.ShapeDtypeStruct((2, rows, part), embed.dtype)] * 4,
        compiler_params=params(),
        cost_estimate=small(),
        name="quarters",
    )(where, embed, other)


def project(pieces, key_weight, value_weight, where, positions):
    rows, half = pieces[0].shape
    columns, width = key_weight.shape
    rows_long, rows_short = positions // 4, positions // 32

    def body(where_ref, *refs):
        piece_refs, (key_ref, value_ref, mine_ref, sent_ref) = refs[:10], refs[10:]
        whole_pieces = [ref[...] for ref in piece_refs]
        lefts, rights = [
            side[:3] + [jnp.concatenate(side[3:], axis=1)]
            for side in (whole_pieces[:5], whole_pieces[5:])
        ]

        def fill(long_ref, short_ref):
            short_ref[4 * rows_short :] = jnp.zeros(
                (positions - 4 * rows_short, 2 * width), jnp.float32
            )
            near = where_ref[2]
            first = pl.ds(pl.multiple_of(near * half, half), half)
            second = pl.ds(pl.multiple_of((1 - near) * half, half), half)
            for i, (left, right) in enumerate(zip(lefts, rights)):
                place = where_ref[0] ^ i
                at_long = pl.ds(pl.multiple_of(place * rows_long, rows_long), rows_long)
                at_short = pl.ds(pl.multiple_of(place * rows_short, rows_short), rows_short)
                for j, ref in enumerate((key_ref, value_ref)):
                    sums = jnp.dot(left, ref[first], preferred_element_type=jnp.float32)
                    sums += jnp.dot(right, ref[second], preferred_element_type=jnp.float32)
                    across = slice(j * width, (j + 1) * width)
                    long_ref[at_long, across] = sums[:rows_long]
                    short_ref[at_short, across] = sums[rows_long:]

        @pl.when(where_ref[1] == 1)
        def _():
            fill(mine_ref, sent_ref)

        @pl.when(where_ref[1] == 0)
        def _():
            fill(sent_ref, mine_ref)

    def whole(*shape):
        return pl.BlockSpec(shape, lambda i, w: (0, 0))

    return pl.pallas_call(
        body,
        grid_spec=pltpu.PrefetchScalarGridSpec(
            num_scalar_prefetch=1,
            grid=(1,),
            in_specs=([whole(rows, half)] * 3 + [whole(rows, half // 2)] * 2) * 2
            + [whole(columns, width)] * 2,
            out_specs=[whole(positions, 2 * width)] * 2,
        ),
        out_shape=[jax.ShapeDtypeStruct((positions, 2 * width), jnp.float32)] * 2,
        compiler_params=params(),
        cost_estimate=pl.CostEstimate(
            flops=7000000000, bytes_accessed=8 * 1024 * 1024, transcendentals=0
        ),
        name="project",
    )(where, *pieces, key_weight, value_weight)


def text_of_pair(embed, key_weight, value_weight, length, encoder, n, before, between, after):
    positions, columns = embed.shape
    core = lax.axis_index("dp")
    me = lax.axis_index("seq")
    half = columns // 2
    other = swap(embed)
    other_facts = swap(jnp.stack([length, encoder]))
    mine_long = length > other_facts[0]
    encoder_long = jnp.where(mine_long, encoder, other_facts[1])
    encoder_short = jnp.where(mine_long, other_facts[1], encoder)
    rows_long, rows_short = positions // 4, positions // 32
    rows = rows_long + rows_short
    place = me & 3
    is_long = mine_long.astype(jnp.int32)
    send_a, part_a, send_b, part_b = quarters(embed, other, jnp.stack([core, is_long, place]))
    on_row = lax.broadcasted_iota(jnp.int32, (rows, 1), 0)
    apart = jnp.where(on_row < rows_long, encoder_long, encoder_short) ^ me
    x, y = me & 1, (me >> 1) & 1

    def choose(own, got, bit):
        return jnp.where((apart >> bit) & 1 == 0, own, got)

    part_a = choose(part_a, exchange(send_a, 1, n), 0)
    part_b = choose(part_b, exchange(send_b, 2, n), 1)
    got_a = exchange(pick(part_a, 1 - y), 2, n)
    got_b = exchange(pick(part_b, 1 - x), 1, n)
    piece = jnp.concatenate(
        [choose(pick(part_a, y), got_a, 1), choose(pick(part_b, x), got_b, 0)], axis=1
    )
    last = n.bit_length() - 2
    for bit in range(2, last):
        piece = choose(piece, exchange(piece, 1 << bit, n), bit)
    near = (me >> 2) & 1
    own = jnp.where(near == 0, piece[:, : half // 2], piece[:, half // 2 :])
    own = before(own)
    own = between(choose(own, exchange(own, 1 << last, n), last))
    far, own_x, own_y = exchange(own, 4, n), exchange(own, 1, n), exchange(own, 2, n)
    pieces = []
    for here, at_x, at_y in (
        (own, own_x, own_y),
        (far, exchange(far, 1, n), after(exchange(far, 2, n))),
    ):
        across_a = exchange(at_y[:, : half // 4], 1, n)
        across_b = exchange(at_x[:, half // 4 :], 2, n)
        pieces += [here, at_x, at_y, across_a, across_b]
    mine, other_sums = project(
        pieces, key_weight, value_weight, jnp.stack([place, is_long, near]), positions
    )
    return (mine + swap(other_sums)).astype(jnp.bfloat16)


def text_of_clip(embed, key_weight, value_weight, encoder):
    kept = jnp.where(lax.axis_index("seq") == encoder, embed, 0).astype(embed.dtype)
    prompt = lax.psum(kept, "seq")
    weight = lax.all_gather(
        jnp.concatenate([key_weight, value_weight], axis=1), "dp", axis=0, tiled=True
    )
    return jnp.dot(prompt, weight, preferred_element_type=jnp.float32).astype(jnp.bfloat16)


def shards(
    n_dp,
    n,
    self_query,
    self_key,
    self_value,
    cross_query,
    text_embed,
    cross_key_weight,
    cross_value_weight,
    text_lengths,
    encoder_index,
):
    heads = cross_key_weight.shape[1] // HEAD
    inputs = [self_query[0], self_key[0], self_value[0], cross_query[0]]
    embed, weights = text_embed[0, 0], (cross_key_weight, cross_value_weight)
    if n_dp != 2 or n < 16 or n & (n - 1) or heads % 2:
        blocks = spread(pack(inputs, n, [(a, 0) for a in range(4)], heads * HEAD))
        text = text_of_clip(embed, *weights, encoder_index[0])
        self_out = self_attention(blocks, 0)
        out = cross_attention(blocks, 3, text, 0, text_lengths, self_out)
        return unpack([spread(out)])[None]

    part = heads // 2 * HEAD
    place = lax.axis_index("seq") & (QUAD - 1)
    lines = spread_lines(pack(inputs, n, [(a, 0) for a in range(4)], part))
    cross_second = pack(inputs, n, [(3, 1)], part)
    lines, cross_second = lax.optimization_barrier((lines, cross_second))
    cross_second = spread(cross_second)
    earlier = spread_planes(lines[:, :3], place)
    cross_first = spread_planes(lines[:, 3:], place)
    rest = pack(inputs, n, [(a, 1) for a in range(3)], part)
    self_first = later = None

    def before(piece):
        nonlocal cross_second
        piece, cross_second = lax.optimization_barrier((piece, cross_second))
        return piece

    def between(piece):
        nonlocal rest, earlier, self_first, later
        piece, rest, earlier = lax.optimization_barrier((piece, rest, earlier))
        self_first = self_attention(earlier, 0, place)
        later = spread(rest)
        return piece

    def after(piece):
        nonlocal self_first
        piece, self_first = lax.optimization_barrier((piece, self_first))
        return piece

    text = text_of_pair(
        embed, *weights, text_lengths[0], encoder_index[0], n, before, between, after
    )
    out = cross_attention(cross_first, 0, text, 0, text_lengths, self_first, place)
    later, out = lax.optimization_barrier((later, out))
    tokens = spread(out)
    self_second = self_attention(later, 0)
    out = cross_attention(cross_second, 0, text, heads // 2, text_lengths, self_second)
    tokens, out = lax.optimization_barrier((tokens, out))
    return unpack([tokens, spread(out)])[None]


def solution(mesh):
    placed = (
        P("dp", "seq", None),
        P("dp", "seq", None),
        P("dp", "seq", None),
        P("dp", "seq", None),
        P("dp", "seq", None, None),
        P("dp", "seq"),
        P("dp", "seq"),
        P("dp"),
        P("dp"),
    )
    return jax.shard_map(
        functools.partial(shards, mesh.shape["dp"], mesh.shape["seq"]),
        mesh=mesh,
        in_specs=placed,
        out_specs=P("dp", "seq", None),
        check_vma=False,
    )
```

```python
import functools
import math

import jax
import jax.numpy as jnp
from jax import lax
from jax.experimental import pallas as pl
from jax.experimental.pallas import tpu as pltpu
from jax.sharding import PartitionSpec as P

HEAD = 128
QUAD = 4
LOG2E = math.log2(math.e)


def params(mebibytes=48):
    return pltpu.CompilerParams(vmem_limit_bytes=mebibytes * 1024 * 1024)


def small():
    return pl.CostEstimate(flops=0, bytes_accessed=4 * 1024 * 1024, transcendentals=0)


def pack(arrays, n, items, part):
    rows, columns = arrays[0].shape
    groups = columns // n // part
    per = max(1, n // 4)
    count = len(items)

    def body(*refs):
        for j in range(per):
            for i in range(count):
                refs[-1][j, i] = refs[j * count + i][...]

    def block(j, g):
        return pl.BlockSpec((rows, part), lambda i: (0, (i * per + j) * groups + g))

    return pl.pallas_call(
        body,
        grid=(n // per,),
        in_specs=[block(j, g) for j in range(per) for _, g in items],
        out_specs=pl.BlockSpec((per, count, rows, part), lambda i: (i, 0, 0, 0)),
        out_shape=jax.ShapeDtypeStruct((n, count, rows, part), arrays[0].dtype),
        compiler_params=params(60),
        cost_estimate=small(),
        name="pack",
    )(*[arrays[a] for _ in range(per) for a, _ in items])


def unpack(parts):
    groups = len(parts)
    n, rows, part = parts[0].shape
    width = part * groups
    per = max(1, n // 4)

    def body(*refs):
        for g in range(groups):
            for j in range(per):
                start = j * width + g * part
                refs[groups][:, start : start + part] = refs[g][j]

    return pl.pallas_call(
        body,
        grid=(n // per,),
        in_specs=[pl.BlockSpec((per, rows, part), lambda i: (i, 0, 0))] * groups,
        out_specs=pl.BlockSpec((rows, per * width), lambda i: (0, i)),
        out_shape=jax.ShapeDtypeStruct((rows, n * width), parts[0].dtype),
        compiler_params=params(),
        cost_estimate=small(),
        name="unpack",
    )(*parts)


def self_attention(blocks, first, place=None):
    n, _, rows, width = blocks.shape
    heads = width // HEAD
    tokens = n * rows
    per = max(1, min(n, 256 // rows))
    factor = LOG2E / HEAD**0.5
    turned = place is not None
    step = n if turned else min(n, 16)
    shape = (n // QUAD, QUAD) if turned else (n,)

    def body(place_ref, q_ref, k_ref, v_ref, out_ref, values):
        @pl.when(pl.program_id(1) == 0)
        def _():
            values[:, :HEAD] = v_ref[:, 0].reshape(tokens, HEAD)
            values[:, HEAD:] = jnp.ones((tokens, HEAD), jnp.bfloat16)

        keys = k_ref[:, 0].reshape(tokens, HEAD)
        for at in range(0, step, per):
            q = q_ref[at : at + per, 0].reshape(per * rows, HEAD)
            scores = lax.dot_general(
                q, keys, (((1,), (1,)), ((), ())), preferred_element_type=jnp.float32
            )
            top = jnp.max(scores, axis=1, keepdims=True)
            probs = jnp.exp2((scores - top) * factor).astype(jnp.bfloat16)
            total = jnp.dot(probs, values[...], preferred_element_type=jnp.float32)
            out = (total[:, :HEAD] / total[:, HEAD:]).astype(jnp.bfloat16).reshape(per, rows, HEAD)
            if turned:
                r, z = divmod(at, n // QUAD)
                out_ref[z : z + per, r ^ place_ref[0]] = out
            else:
                out_ref[at : at + per] = out

    if turned:
        out_block = pl.BlockSpec((*shape, rows, HEAD), lambda h, i, _: (0, 0, 0, h))
    else:
        out_block = pl.BlockSpec((step, rows, HEAD), lambda h, i, _: (i, 0, h))
    return pl.pallas_call(
        body,
        grid_spec=pltpu.PrefetchScalarGridSpec(
            num_scalar_prefetch=1,
            grid=(heads, n // step),
            in_specs=[
                pl.BlockSpec((step, 1, rows, HEAD), lambda h, i, _: (i, first, 0, h)),
                pl.BlockSpec((n, 1, rows, HEAD), lambda h, i, _: (0, first + 1, 0, h)),
                pl.BlockSpec((n, 1, rows, HEAD), lambda h, i, _: (0, first + 2, 0, h)),
            ],
            out_specs=out_block,
            scratch_shapes=[pltpu.VMEM((tokens, 2 * HEAD), jnp.bfloat16)],
        ),
        out_shape=jax.ShapeDtypeStruct((*shape, rows, width), jnp.bfloat16),
        compiler_params=params(),
        cost_estimate=pl.CostEstimate(
            flops=16 * heads * tokens * tokens * HEAD,
            bytes_accessed=2 * 4 * tokens * width,
            transcendentals=heads * tokens * tokens,
        ),
        name="self_attention",
    )(
        place.reshape(1) if turned else jnp.zeros(1, jnp.int32), blocks, blocks, blocks
    ).reshape(n, rows, width)


def cross_attention(blocks, item, text, head, length, self_out, place=None):
    n, _, rows, width = blocks.shape
    heads = width // HEAD
    positions = text.shape[0]
    values_at = text.shape[1] // HEAD // 2 + head
    factor = LOG2E / HEAD**0.5
    turned = place is not None
    shape = (n // QUAD, QUAD) if turned else (n,)

    def body(length_ref, place_ref, q_ref, k_ref, v_ref, self_ref, out_ref, values):
        values[:, :HEAD] = v_ref[...]
        values[:, HEAD:] = jnp.ones((positions, HEAD), jnp.bfloat16)
        valid = lax.broadcasted_iota(jnp.int32, (1, positions), 1) < length_ref[0]
        for at in range(n):
            scores = lax.dot_general(
                q_ref[at, 0],
                k_ref[...],
                (((1,), (1,)), ((), ())),
                preferred_element_type=jnp.float32,
            )
            scores = jnp.where(valid, scores, -1e30)
            top = jnp.max(scores, axis=1, keepdims=True)
            probs = jnp.exp2((scores - top) * factor).astype(jnp.bfloat16)
            total = jnp.dot(probs, values[...], preferred_element_type=jnp.float32)
            out = (total[:, :HEAD] / total[:, HEAD:]).astype(jnp.bfloat16).astype(jnp.float32)
            r, z = divmod(at, n // QUAD)
            block = (z, r ^ place_ref[0]) if turned else at
            out_ref[block] = (out + self_ref[block].astype(jnp.float32)).astype(jnp.bfloat16)

    whole = pl.BlockSpec((*shape, rows, HEAD), lambda h, *_: (0,) * len(shape) + (0, h))
    return pl.pallas_call(
        body,
        grid_spec=pltpu.PrefetchScalarGridSpec(
            num_scalar_prefetch=2,
            grid=(heads,),
            in_specs=[
                pl.BlockSpec((n, 1, rows, HEAD), lambda h, *_: (0, item, 0, h)),
                pl.BlockSpec((positions, HEAD), lambda h, *_: (0, head + h)),
                pl.BlockSpec((positions, HEAD), lambda h, *_: (0, values_at + h)),
                whole,
            ],
            out_specs=whole,
            scratch_shapes=[pltpu.VMEM((positions, 2 * HEAD), jnp.bfloat16)],
        ),
        out_shape=jax.ShapeDtypeStruct((*shape, rows, width), jnp.bfloat16),
        compiler_params=params(),
        cost_estimate=pl.CostEstimate(
            flops=32 * heads * n * rows * positions * HEAD,
            bytes_accessed=2 * 3 * n * rows * width,
            transcendentals=heads * n * rows * positions,
        ),
        name="cross_attention",
    )(
        length,
        place.reshape(1) if turned else jnp.zeros(1, jnp.int32),
        blocks,
        text,
        text,
        self_out.reshape(*shape, rows, width),
    ).reshape(n, rows, width)


def spread(blocks, groups=None):
    flat = blocks.reshape(blocks.shape[0], -1, blocks.shape[-1])
    return lax.all_to_all(
        flat, "seq", split_axis=0, concat_axis=0, tiled=True, axis_index_groups=groups
    ).reshape(blocks.shape)


def spread_lines(blocks):
    n = blocks.shape[0]
    return spread(blocks, [[q + QUAD * z for z in range(n // QUAD)] for q in range(QUAD)])


def join(parts):
    count = len(parts)
    planes, *rest = parts[0].shape

    def body(*refs):
        for i in range(count):
            refs[count][i] = refs[i][...]

    return pl.pallas_call(
        body,
        grid=(planes,),
        in_specs=[pl.BlockSpec((1, *rest), lambda i: (i, 0, 0, 0))] * count,
        out_specs=pl.BlockSpec((count, 1, *rest), lambda i: (0, i, 0, 0, 0)),
        out_shape=jax.ShapeDtypeStruct((count, planes, *rest), parts[0].dtype),
        compiler_params=params(),
        cost_estimate=pl.CostEstimate(
            flops=10000000000, bytes_accessed=4 * 1024 * 1024, transcendentals=0
        ),
        name="join",
    )(*parts).reshape(count * planes, *rest)


def spread_planes(blocks, place, first, count):
    n, items, rows, width = blocks.shape
    lines = blocks.reshape(n // QUAD, QUAD, items, rows, width)
    parts = []
    for r in range(QUAD):
        part = lax.dynamic_slice(
            lines, (0, place ^ r, first, 0, 0), (n // QUAD, 1, count, rows, width)
        )[:, 0]
        parts.append(exchange(part, r, n) if r else part)
    return parts


def exchange(value, apart, n):
    return lax.ppermute(value, "seq", [(i, i ^ apart) for i in range(n)])


def pick(value, index):
    return lax.dynamic_index_in_dim(value, index, 0, keepdims=False)


def swap(value):
    return lax.ppermute(value, "dp", [(0, 1), (1, 0)])


def quarters(embed, other, where):
    positions, columns = embed.shape
    rows_long, rows_short = positions // 4, positions // 32
    rows = rows_long + rows_short
    half, part = columns // 2, columns // 4

    def body(where_ref, own_ref, other_ref, send_a, keep_a, send_b, keep_b):
        x, y = where_ref[2] & 1, where_ref[2] >> 1

        def fill(long_ref, short_ref):
            for i in range(2):
                for ref, place, first in (
                    (send_a, 2 * i + 1 - x, 0),
                    (keep_a, 2 * i + x, 0),
                    (send_b, 2 * (1 - y) + i, part),
                    (keep_b, 2 * y + i, part),
                ):
                    across = slice(first, first + part)
                    at_long = pl.ds(pl.multiple_of(place * rows_long, rows_long), rows_long)
                    at_short = pl.ds(pl.multiple_of(place * rows_short, rows_short), rows_short)
                    ref[i, :rows_long] = long_ref[at_long, across]
                    ref[i, rows_long:] = short_ref[at_short, across]

        @pl.when(where_ref[1] == 1)
        def _():
            fill(own_ref, other_ref)

        @pl.when(where_ref[1] == 0)
        def _():
            fill(other_ref, own_ref)

    return pl.pallas_call(
        body,
        grid_spec=pltpu.PrefetchScalarGridSpec(
            num_scalar_prefetch=1,
            grid=(1,),
            in_specs=[pl.BlockSpec((positions, half), lambda i, w: (0, w[0]))] * 2,
            out_specs=[pl.BlockSpec((2, rows, part), lambda i, w: (0, 0, 0))] * 4,
        ),
        out_shape=[jax.ShapeDtypeStruct((2, rows, part), embed.dtype)] * 4,
        compiler_params=params(),
        cost_estimate=small(),
        name="quarters",
    )(where, embed, other)


def project(pieces, key_weight, value_weight, where, positions):
    rows, half = pieces[0].shape
    columns, width = key_weight.shape
    rows_long, rows_short = positions // 4, positions // 32

    def body(where_ref, *refs):
        piece_refs, (key_ref, value_ref, mine_ref, sent_ref) = refs[:10], refs[10:]
        whole_pieces = [ref[...] for ref in piece_refs]
        lefts, rights = [
            side[:3] + [jnp.concatenate(side[3:], axis=1)]
            for side in (whole_pieces[:5], whole_pieces[5:])
        ]

        def fill(long_ref, short_ref):
            short_ref[4 * rows_short :] = jnp.zeros(
                (positions - 4 * rows_short, 2 * width), jnp.float32
            )
            near = where_ref[2]
            first = pl.ds(pl.multiple_of(near * half, half), half)
            second = pl.ds(pl.multiple_of((1 - near) * half, half), half)
            for i, (left, right) in enumerate(zip(lefts, rights)):
                place = where_ref[0] ^ i
                at_long = pl.ds(pl.multiple_of(place * rows_long, rows_long), rows_long)
                at_short = pl.ds(pl.multiple_of(place * rows_short, rows_short), rows_short)
                for j, ref in enumerate((key_ref, value_ref)):
                    sums = jnp.dot(left, ref[first], preferred_element_type=jnp.float32)
                    sums += jnp.dot(right, ref[second], preferred_element_type=jnp.float32)
                    across = slice(j * width, (j + 1) * width)
                    long_ref[at_long, across] = sums[:rows_long]
                    short_ref[at_short, across] = sums[rows_long:]

        @pl.when(where_ref[1] == 1)
        def _():
            fill(mine_ref, sent_ref)

        @pl.when(where_ref[1] == 0)
        def _():
            fill(sent_ref, mine_ref)

    def whole(*shape):
        return pl.BlockSpec(shape, lambda i, w: (0, 0))

    return pl.pallas_call(
        body,
        grid_spec=pltpu.PrefetchScalarGridSpec(
            num_scalar_prefetch=1,
            grid=(1,),
            in_specs=([whole(rows, half)] * 3 + [whole(rows, half // 2)] * 2) * 2
            + [whole(columns, width)] * 2,
            out_specs=[whole(positions, 2 * width)] * 2,
        ),
        out_shape=[jax.ShapeDtypeStruct((positions, 2 * width), jnp.float32)] * 2,
        compiler_params=params(),
        cost_estimate=pl.CostEstimate(
            flops=16000000000, bytes_accessed=8 * 1024 * 1024, transcendentals=0
        ),
        name="project",
    )(where, *pieces, key_weight, value_weight)


def text_of_pair(embed, key_weight, value_weight, length, encoder, n, between, after):
    positions, columns = embed.shape
    core = lax.axis_index("dp")
    me = lax.axis_index("seq")
    half = columns // 2
    other = swap(embed)
    other_facts = swap(jnp.stack([length, encoder]))
    mine_long = length > other_facts[0]
    encoder_long = jnp.where(mine_long, encoder, other_facts[1])
    encoder_short = jnp.where(mine_long, other_facts[1], encoder)
    rows_long, rows_short = positions // 4, positions // 32
    rows = rows_long + rows_short
    place = me & 3
    is_long = mine_long.astype(jnp.int32)
    send_a, part_a, send_b, part_b = quarters(embed, other, jnp.stack([core, is_long, place]))
    on_row = lax.broadcasted_iota(jnp.int32, (rows, 1), 0)
    apart = jnp.where(on_row < rows_long, encoder_long, encoder_short) ^ me
    x, y = me & 1, (me >> 1) & 1

    def choose(own, got, bit):
        return jnp.where((apart >> bit) & 1 == 0, own, got)

    part_a = choose(part_a, exchange(send_a, 1, n), 0)
    part_b = choose(part_b, exchange(send_b, 2, n), 1)
    got_a = exchange(pick(part_a, 1 - y), 2, n)
    got_b = exchange(pick(part_b, 1 - x), 1, n)
    piece = jnp.concatenate(
        [choose(pick(part_a, y), got_a, 1), choose(pick(part_b, x), got_b, 0)], axis=1
    )
    last = n.bit_length() - 2
    for bit in range(2, last):
        piece = choose(piece, exchange(piece, 1 << bit, n), bit)
    near = (me >> 2) & 1
    own = jnp.where(near == 0, piece[:, : half // 2], piece[:, half // 2 :])
    own = between(choose(own, exchange(own, 1 << last, n), last))
    far, own_x, own_y = exchange(own, 4, n), exchange(own, 1, n), exchange(own, 2, n)
    pieces = []
    for here, at_x, at_y in (
        (own, own_x, own_y),
        (far, exchange(far, 1, n), after(exchange(far, 2, n))),
    ):
        across_a = exchange(at_y[:, : half // 4], 1, n)
        across_b = exchange(at_x[:, half // 4 :], 2, n)
        pieces += [here, at_x, at_y, across_a, across_b]
    mine, other_sums = project(
        pieces, key_weight, value_weight, jnp.stack([place, is_long, near]), positions
    )
    return (mine + swap(other_sums)).astype(jnp.bfloat16)


def text_of_clip(embed, key_weight, value_weight, encoder):
    kept = jnp.where(lax.axis_index("seq") == encoder, embed, 0).astype(embed.dtype)
    prompt = lax.psum(kept, "seq")
    weight = lax.all_gather(
        jnp.concatenate([key_weight, value_weight], axis=1), "dp", axis=0, tiled=True
    )
    return jnp.dot(prompt, weight, preferred_element_type=jnp.float32).astype(jnp.bfloat16)


def shards(
    n_dp,
    n,
    self_query,
    self_key,
    self_value,
    cross_query,
    text_embed,
    cross_key_weight,
    cross_value_weight,
    text_lengths,
    encoder_index,
):
    heads = cross_key_weight.shape[1] // HEAD
    inputs = [self_query[0], self_key[0], self_value[0], cross_query[0]]
    embed, weights = text_embed[0, 0], (cross_key_weight, cross_value_weight)
    if n_dp != 2 or n < 16 or n & (n - 1) or heads % 2:
        blocks = spread(pack(inputs, n, [(a, 0) for a in range(4)], heads * HEAD))
        text = text_of_clip(embed, *weights, encoder_index[0])
        self_out = self_attention(blocks, 0)
        out = cross_attention(blocks, 3, text, 0, text_lengths, self_out)
        return unpack([spread(out)])[None]

    part = heads // 2 * HEAD
    place = lax.axis_index("seq") & (QUAD - 1)
    lines = pack(inputs, n, [(a, 0) for a in range(4)], part)
    lines, embed = lax.optimization_barrier((lines, embed))
    lines = spread_lines(lines)
    earlier = join(spread_planes(lines, place, 0, 3))
    cross_first = join(spread_planes(lines, place, 3, 1))
    rest = pack(inputs, n, [(a, 1) for a in range(4)], part)
    self_first = later = None

    def between(piece):
        nonlocal rest, earlier, self_first, later
        piece, rest, earlier = lax.optimization_barrier((piece, rest, earlier))
        self_first = self_attention(earlier, 0, place)
        later = spread(rest)
        return piece

    def after(piece):
        nonlocal self_first
        piece, self_first = lax.optimization_barrier((piece, self_first))
        return piece

    text = text_of_pair(
        embed, *weights, text_lengths[0], encoder_index[0], n, between, after
    )
    out = cross_attention(cross_first, 0, text, 0, text_lengths, self_first, place)
    later, out = lax.optimization_barrier((later, out))
    tokens = spread(out)
    self_second = self_attention(later, 0)
    out = cross_attention(later, 3, text, heads // 2, text_lengths, self_second)
    tokens, out = lax.optimization_barrier((tokens, out))
    return unpack([tokens, spread(out)])[None]


def solution(mesh):
    placed = (
        P("dp", "seq", None),
        P("dp", "seq", None),
        P("dp", "seq", None),
        P("dp", "seq", None),
        P("dp", "seq", None, None),
        P("dp", "seq"),
        P("dp", "seq"),
        P("dp"),
        P("dp"),
    )
    return jax.shard_map(
        functools.partial(shards, mesh.shape["dp"], mesh.shape["seq"]),
        mesh=mesh,
        in_specs=placed,
        out_specs=P("dp", "seq", None),
        check_vma=False,
    )
```

```python
import functools
import math

import jax
import jax.numpy as jnp
from jax import lax
from jax.experimental import pallas as pl
from jax.experimental.pallas import tpu as pltpu
from jax.sharding import PartitionSpec as P

HEAD = 128
QUAD = 4
LOG2E = math.log2(math.e)


def params(mebibytes=48):
    return pltpu.CompilerParams(vmem_limit_bytes=mebibytes * 1024 * 1024)


def small():
    return pl.CostEstimate(flops=0, bytes_accessed=4 * 1024 * 1024, transcendentals=0)


def pack(arrays, n, items, part):
    rows, columns = arrays[0].shape
    groups = columns // n // part
    per = max(1, n // 4)
    count = len(items)

    def body(*refs):
        for j in range(per):
            for i in range(count):
                refs[-1][j, i] = refs[j * count + i][...]

    def block(j, g):
        return pl.BlockSpec((rows, part), lambda i: (0, (i * per + j) * groups + g))

    return pl.pallas_call(
        body,
        grid=(n // per,),
        in_specs=[block(j, g) for j in range(per) for _, g in items],
        out_specs=pl.BlockSpec((per, count, rows, part), lambda i: (i, 0, 0, 0)),
        out_shape=jax.ShapeDtypeStruct((n, count, rows, part), arrays[0].dtype),
        compiler_params=params(60),
        cost_estimate=small(),
        name="pack",
    )(*[arrays[a] for _ in range(per) for a, _ in items])


def unpack(parts):
    groups = len(parts)
    n, rows, part = parts[0].shape
    width = part * groups
    per = max(1, n // 4)

    def body(*refs):
        for g in range(groups):
            for j in range(per):
                start = j * width + g * part
                refs[groups][:, start : start + part] = refs[g][j]

    return pl.pallas_call(
        body,
        grid=(n // per,),
        in_specs=[pl.BlockSpec((per, rows, part), lambda i: (i, 0, 0))] * groups,
        out_specs=pl.BlockSpec((rows, per * width), lambda i: (0, i)),
        out_shape=jax.ShapeDtypeStruct((rows, n * width), parts[0].dtype),
        compiler_params=params(),
        cost_estimate=small(),
        name="unpack",
    )(*parts)


def self_attention(blocks, first, place=None):
    n, _, rows, width = blocks.shape
    heads = width // HEAD
    tokens = n * rows
    per = max(1, min(n, 256 // rows))
    factor = LOG2E / HEAD**0.5
    turned = place is not None
    step = n if turned else min(n, 16)
    shape = (n // QUAD, QUAD) if turned else (n,)

    def body(place_ref, q_ref, k_ref, v_ref, out_ref, values):
        @pl.when(pl.program_id(1) == 0)
        def _():
            values[:, :HEAD] = v_ref[:, 0].reshape(tokens, HEAD)
            values[:, HEAD:] = jnp.ones((tokens, HEAD), jnp.bfloat16)

        keys = k_ref[:, 0].reshape(tokens, HEAD)
        for at in range(0, step, per):
            q = q_ref[at : at + per, 0].reshape(per * rows, HEAD)
            scores = lax.dot_general(
                q, keys, (((1,), (1,)), ((), ())), preferred_element_type=jnp.float32
            )
            top = jnp.max(scores, axis=1, keepdims=True)
            probs = jnp.exp2((scores - top) * factor).astype(jnp.bfloat16)
            total = jnp.dot(probs, values[...], preferred_element_type=jnp.float32)
            out = (total[:, :HEAD] / total[:, HEAD:]).astype(jnp.bfloat16).reshape(per, rows, HEAD)
            if turned:
                r, z = divmod(at, n // QUAD)
                out_ref[z : z + per, r ^ place_ref[0]] = out
            else:
                out_ref[at : at + per] = out

    if turned:
        out_block = pl.BlockSpec((*shape, rows, HEAD), lambda h, i, _: (0, 0, 0, h))
    else:
        out_block = pl.BlockSpec((step, rows, HEAD), lambda h, i, _: (i, 0, h))
    return pl.pallas_call(
        body,
        grid_spec=pltpu.PrefetchScalarGridSpec(
            num_scalar_prefetch=1,
            grid=(heads, n // step),
            in_specs=[
                pl.BlockSpec((step, 1, rows, HEAD), lambda h, i, _: (i, first, 0, h)),
                pl.BlockSpec((n, 1, rows, HEAD), lambda h, i, _: (0, first + 1, 0, h)),
                pl.BlockSpec((n, 1, rows, HEAD), lambda h, i, _: (0, first + 2, 0, h)),
            ],
            out_specs=out_block,
            scratch_shapes=[pltpu.VMEM((tokens, 2 * HEAD), jnp.bfloat16)],
        ),
        out_shape=jax.ShapeDtypeStruct((*shape, rows, width), jnp.bfloat16),
        compiler_params=params(),
        cost_estimate=pl.CostEstimate(
            flops=16 * heads * tokens * tokens * HEAD,
            bytes_accessed=2 * 4 * tokens * width,
            transcendentals=heads * tokens * tokens,
        ),
        name="self_attention",
    )(
        place.reshape(1) if turned else jnp.zeros(1, jnp.int32), blocks, blocks, blocks
    ).reshape(n, rows, width)


def cross_attention(blocks, item, text, head, length, self_out, place=None):
    n, _, rows, width = blocks.shape
    heads = width // HEAD
    positions = text.shape[0]
    values_at = text.shape[1] // HEAD // 2 + head
    factor = LOG2E / HEAD**0.5
    turned = place is not None
    shape = (n // QUAD, QUAD) if turned else (n,)

    def body(length_ref, place_ref, q_ref, k_ref, v_ref, self_ref, out_ref, values):
        values[:, :HEAD] = v_ref[...]
        values[:, HEAD:] = jnp.ones((positions, HEAD), jnp.bfloat16)
        valid = lax.broadcasted_iota(jnp.int32, (1, positions), 1) < length_ref[0]
        for at in range(n):
            scores = lax.dot_general(
                q_ref[at, 0],
                k_ref[...],
                (((1,), (1,)), ((), ())),
                preferred_element_type=jnp.float32,
            )
            scores = jnp.where(valid, scores, -1e30)
            top = jnp.max(scores, axis=1, keepdims=True)
            probs = jnp.exp2((scores - top) * factor).astype(jnp.bfloat16)
            total = jnp.dot(probs, values[...], preferred_element_type=jnp.float32)
            out = (total[:, :HEAD] / total[:, HEAD:]).astype(jnp.bfloat16).astype(jnp.float32)
            r, z = divmod(at, n // QUAD)
            block = (z, r ^ place_ref[0]) if turned else at
            out_ref[block] = (out + self_ref[block].astype(jnp.float32)).astype(jnp.bfloat16)

    whole = pl.BlockSpec((*shape, rows, HEAD), lambda h, *_: (0,) * len(shape) + (0, h))
    return pl.pallas_call(
        body,
        grid_spec=pltpu.PrefetchScalarGridSpec(
            num_scalar_prefetch=2,
            grid=(heads,),
            in_specs=[
                pl.BlockSpec((n, 1, rows, HEAD), lambda h, *_: (0, item, 0, h)),
                pl.BlockSpec((positions, HEAD), lambda h, *_: (0, head + h)),
                pl.BlockSpec((positions, HEAD), lambda h, *_: (0, values_at + h)),
                whole,
            ],
            out_specs=whole,
            scratch_shapes=[pltpu.VMEM((positions, 2 * HEAD), jnp.bfloat16)],
        ),
        out_shape=jax.ShapeDtypeStruct((*shape, rows, width), jnp.bfloat16),
        compiler_params=params(),
        cost_estimate=pl.CostEstimate(
            flops=32 * heads * n * rows * positions * HEAD,
            bytes_accessed=2 * 3 * n * rows * width,
            transcendentals=heads * n * rows * positions,
        ),
        name="cross_attention",
    )(
        length,
        place.reshape(1) if turned else jnp.zeros(1, jnp.int32),
        blocks,
        text,
        text,
        self_out.reshape(*shape, rows, width),
    ).reshape(n, rows, width)


def spread(blocks, groups=None):
    flat = blocks.reshape(blocks.shape[0], -1, blocks.shape[-1])
    return lax.all_to_all(
        flat, "seq", split_axis=0, concat_axis=0, tiled=True, axis_index_groups=groups
    ).reshape(blocks.shape)


def spread_lines(blocks):
    n = blocks.shape[0]
    return spread(blocks, [[q + QUAD * z for z in range(n // QUAD)] for q in range(QUAD)])


def join(parts):
    count = len(parts)
    planes, *rest = parts[0].shape

    def body(*refs):
        for i in range(count):
            refs[count][i] = refs[i][...]

    return pl.pallas_call(
        body,
        grid=(planes,),
        in_specs=[pl.BlockSpec((1, *rest), lambda i: (i, 0, 0, 0))] * count,
        out_specs=pl.BlockSpec((count, 1, *rest), lambda i: (0, i, 0, 0, 0)),
        out_shape=jax.ShapeDtypeStruct((count, planes, *rest), parts[0].dtype),
        compiler_params=params(),
        cost_estimate=pl.CostEstimate(
            flops=10000000000, bytes_accessed=4 * 1024 * 1024, transcendentals=0
        ),
        name="join",
    )(*parts).reshape(count * planes, *rest)


def spread_planes(blocks, place, first, count):
    n, items, rows, width = blocks.shape
    lines = blocks.reshape(n // QUAD, QUAD, items, rows, width)
    parts = []
    for r in range(QUAD):
        part = lax.dynamic_slice(
            lines, (0, place ^ r, first, 0, 0), (n // QUAD, 1, count, rows, width)
        )[:, 0]
        parts.append(exchange(part, r, n) if r else part)
    return parts


def exchange(value, apart, n):
    return lax.ppermute(value, "seq", [(i, i ^ apart) for i in range(n)])


def pick(value, index):
    return lax.dynamic_index_in_dim(value, index, 0, keepdims=False)


def swap(value):
    return lax.ppermute(value, "dp", [(0, 1), (1, 0)])


def quarters(embed, other, where):
    positions, columns = embed.shape
    rows_long, rows_short = positions // 4, positions // 32
    rows = rows_long + rows_short
    half, part = columns // 2, columns // 4

    def body(where_ref, own_ref, other_ref, send_a, keep_a, send_b, keep_b):
        x, y = where_ref[2] & 1, where_ref[2] >> 1

        def fill(long_ref, short_ref):
            for i in range(2):
                for ref, place, first in (
                    (send_a, 2 * i + 1 - x, 0),
                    (keep_a, 2 * i + x, 0),
                    (send_b, 2 * (1 - y) + i, part),
                    (keep_b, 2 * y + i, part),
                ):
                    across = slice(first, first + part)
                    at_long = pl.ds(pl.multiple_of(place * rows_long, rows_long), rows_long)
                    at_short = pl.ds(pl.multiple_of(place * rows_short, rows_short), rows_short)
                    ref[i, :rows_long] = long_ref[at_long, across]
                    ref[i, rows_long:] = short_ref[at_short, across]

        @pl.when(where_ref[1] == 1)
        def _():
            fill(own_ref, other_ref)

        @pl.when(where_ref[1] == 0)
        def _():
            fill(other_ref, own_ref)

    return pl.pallas_call(
        body,
        grid_spec=pltpu.PrefetchScalarGridSpec(
            num_scalar_prefetch=1,
            grid=(1,),
            in_specs=[pl.BlockSpec((positions, half), lambda i, w: (0, w[0]))] * 2,
            out_specs=[pl.BlockSpec((2, rows, part), lambda i, w: (0, 0, 0))] * 4,
        ),
        out_shape=[jax.ShapeDtypeStruct((2, rows, part), embed.dtype)] * 4,
        compiler_params=params(),
        cost_estimate=small(),
        name="quarters",
    )(where, embed, other)


def project(pieces, key_weight, value_weight, where, positions):
    rows, half = pieces[0].shape
    columns, width = key_weight.shape
    rows_long, rows_short = positions // 4, positions // 32

    def body(where_ref, *refs):
        piece_refs, (key_ref, value_ref, mine_ref, sent_ref) = refs[:10], refs[10:]
        whole_pieces = [ref[...] for ref in piece_refs]
        lefts, rights = [
            side[:3] + [jnp.concatenate(side[3:], axis=1)]
            for side in (whole_pieces[:5], whole_pieces[5:])
        ]

        def fill(long_ref, short_ref):
            short_ref[4 * rows_short :] = jnp.zeros(
                (positions - 4 * rows_short, 2 * width), jnp.float32
            )
            near = where_ref[2]
            first = pl.ds(pl.multiple_of(near * half, half), half)
            second = pl.ds(pl.multiple_of((1 - near) * half, half), half)
            for i, (left, right) in enumerate(zip(lefts, rights)):
                place = where_ref[0] ^ i
                at_long = pl.ds(pl.multiple_of(place * rows_long, rows_long), rows_long)
                at_short = pl.ds(pl.multiple_of(place * rows_short, rows_short), rows_short)
                for j, ref in enumerate((key_ref, value_ref)):
                    sums = jnp.dot(left, ref[first], preferred_element_type=jnp.float32)
                    sums += jnp.dot(right, ref[second], preferred_element_type=jnp.float32)
                    across = slice(j * width, (j + 1) * width)
                    long_ref[at_long, across] = sums[:rows_long]
                    short_ref[at_short, across] = sums[rows_long:]

        @pl.when(where_ref[1] == 1)
        def _():
            fill(mine_ref, sent_ref)

        @pl.when(where_ref[1] == 0)
        def _():
            fill(sent_ref, mine_ref)

    def whole(*shape):
        return pl.BlockSpec(shape, lambda i, w: (0, 0))

    return pl.pallas_call(
        body,
        grid_spec=pltpu.PrefetchScalarGridSpec(
            num_scalar_prefetch=1,
            grid=(1,),
            in_specs=([whole(rows, half)] * 3 + [whole(rows, half // 2)] * 2) * 2
            + [whole(columns, width)] * 2,
            out_specs=[whole(positions, 2 * width)] * 2,
        ),
        out_shape=[jax.ShapeDtypeStruct((positions, 2 * width), jnp.float32)] * 2,
        compiler_params=params(),
        cost_estimate=pl.CostEstimate(
            flops=16000000000, bytes_accessed=8 * 1024 * 1024, transcendentals=0
        ),
        name="project",
    )(where, *pieces, key_weight, value_weight)


def text_of_pair(embed, key_weight, value_weight, length, encoder, n, between, after):
    positions, columns = embed.shape
    core = lax.axis_index("dp")
    me = lax.axis_index("seq")
    half = columns // 2
    other = swap(embed)
    other_facts = swap(jnp.stack([length, encoder]))
    mine_long = length > other_facts[0]
    encoder_long = jnp.where(mine_long, encoder, other_facts[1])
    encoder_short = jnp.where(mine_long, other_facts[1], encoder)
    rows_long, rows_short = positions // 4, positions // 32
    rows = rows_long + rows_short
    place = me & 3
    is_long = mine_long.astype(jnp.int32)
    send_a, part_a, send_b, part_b = quarters(embed, other, jnp.stack([core, is_long, place]))
    on_row = lax.broadcasted_iota(jnp.int32, (rows, 1), 0)
    apart = jnp.where(on_row < rows_long, encoder_long, encoder_short) ^ me
    x, y = me & 1, (me >> 1) & 1

    def choose(own, got, bit):
        return jnp.where((apart >> bit) & 1 == 0, own, got)

    part_a = choose(part_a, exchange(send_a, 1, n), 0)
    part_b = choose(part_b, exchange(send_b, 2, n), 1)
    got_a = exchange(pick(part_a, 1 - y), 2, n)
    got_b = exchange(pick(part_b, 1 - x), 1, n)
    piece = jnp.concatenate(
        [choose(pick(part_a, y), got_a, 1), choose(pick(part_b, x), got_b, 0)], axis=1
    )
    last = n.bit_length() - 2
    for bit in range(2, last):
        piece = choose(piece, exchange(piece, 1 << bit, n), bit)
    near = (me >> 2) & 1
    own = jnp.where(near == 0, piece[:, : half // 2], piece[:, half // 2 :])
    own = between(choose(own, exchange(own, 1 << last, n), last))
    far, own_x, own_y = exchange(own, 4, n), exchange(own, 1, n), exchange(own, 2, n)
    pieces = []
    for here, at_x, at_y in (
        (own, own_x, own_y),
        (far, exchange(far, 1, n), after(exchange(far, 2, n))),
    ):
        across_a = exchange(at_y[:, : half // 4], 1, n)
        across_b = exchange(at_x[:, half // 4 :], 2, n)
        pieces += [here, at_x, at_y, across_a, across_b]
    mine, other_sums = project(
        pieces, key_weight, value_weight, jnp.stack([place, is_long, near]), positions
    )
    return (mine + swap(other_sums)).astype(jnp.bfloat16)


def text_of_clip(embed, key_weight, value_weight, encoder):
    kept = jnp.where(lax.axis_index("seq") == encoder, embed, 0).astype(embed.dtype)
    prompt = lax.psum(kept, "seq")
    weight = lax.all_gather(
        jnp.concatenate([key_weight, value_weight], axis=1), "dp", axis=0, tiled=True
    )
    return jnp.dot(prompt, weight, preferred_element_type=jnp.float32).astype(jnp.bfloat16)


def shards(
    n_dp,
    n,
    self_query,
    self_key,
    self_value,
    cross_query,
    text_embed,
    cross_key_weight,
    cross_value_weight,
    text_lengths,
    encoder_index,
):
    heads = cross_key_weight.shape[1] // HEAD
    inputs = [self_query[0], self_key[0], self_value[0], cross_query[0]]
    embed, weights = text_embed[0, 0], (cross_key_weight, cross_value_weight)
    if n_dp != 2 or n < 16 or n & (n - 1) or heads % 2:
        blocks = spread(pack(inputs, n, [(a, 0) for a in range(4)], heads * HEAD))
        text = text_of_clip(embed, *weights, encoder_index[0])
        self_out = self_attention(blocks, 0)
        out = cross_attention(blocks, 3, text, 0, text_lengths, self_out)
        return unpack([spread(out)])[None]

    part = heads // 2 * HEAD
    place = lax.axis_index("seq") & (QUAD - 1)
    lines = spread_lines(pack(inputs, n, [(a, 0) for a in range(4)], part))
    earlier = join(spread_planes(lines, place, 0, 3))
    cross_first = join(spread_planes(lines, place, 3, 1))
    rest = pack(inputs, n, [(a, 1) for a in range(4)], part)
    self_first = later = None

    def between(piece):
        nonlocal rest, earlier, self_first, later
        piece, rest, earlier = lax.optimization_barrier((piece, rest, earlier))
        self_first = self_attention(earlier, 0, place)
        later = spread(rest)
        return piece

    def after(piece):
        nonlocal self_first
        piece, self_first = lax.optimization_barrier((piece, self_first))
        return piece

    text = text_of_pair(
        embed, *weights, text_lengths[0], encoder_index[0], n, between, after
    )
    out = cross_attention(cross_first, 0, text, 0, text_lengths, self_first, place)
    later, out = lax.optimization_barrier((later, out))
    tokens = spread(out)
    self_second = self_attention(later, 0)
    out = cross_attention(later, 3, text, heads // 2, text_lengths, self_second)
    tokens, out = lax.optimization_barrier((tokens, out))
    return unpack([tokens, spread(out)])[None]


def solution(mesh):
    placed = (
        P("dp", "seq", None),
        P("dp", "seq", None),
        P("dp", "seq", None),
        P("dp", "seq", None),
        P("dp", "seq", None, None),
        P("dp", "seq"),
        P("dp", "seq"),
        P("dp"),
        P("dp"),
    )
    return jax.shard_map(
        functools.partial(shards, mesh.shape["dp"], mesh.shape["seq"]),
        mesh=mesh,
        in_specs=placed,
        out_specs=P("dp", "seq", None),
        check_vma=False,
    )
```
